32 devices in a mesh: dom: 1, blk: 4 (over z), grp: 8 (over y, x, core), sub: 1.
Axes of the slice: x: 2, y: 2, z: 4, core: 2. Of those that a mesh axis runs over, the one named last changes fastest.
Arguments:
- records: bfloat16 [512, 8, 1024], P(('dom', 'blk', 'grp')), may hold values from -40 to 40
- flags: int32 [512, 8], P(('dom', 'blk', 'grp')), may hold values 0 or 1
Outputs:
- correlations: bfloat16 [256, 512, 3, 128], P('sub', ('dom', 'blk', 'grp'))
The draws below stay inside these ranges and needn't reach their ends.
All inputs are finite; a program needn't handle non-finite values. No bound on the sum of `flags` on one device may be relied on, other than what follows from the above.
Results may differ from the reference program's by a relative error of at most 0.012.
Values may be sent and summed in bfloat16 or wider, within the bound.
A program may use at most 64 MiB of HBM per device.

```python
import math
import jax
import jax.numpy as jnp
from jax import lax

SEGS = 8
SEG_LEN = 1024
LAGS = 256
STEPS = 3
BINS = 512
BLOCK = 128
CHANNELS = 512
N_BLK = 4
N_SUB = 1


def draw_records(key, part):
    first = jax.random.fold_in(key, 0)
    shape = (CHANNELS, SEGS, SEG_LEN)
    base = jnp.clip(jax.random.normal(first, shape, jnp.float32), -4.0, 4.0)
    colored = base + 0.9 * jnp.roll(base, 1, axis=2) + 0.6 * jnp.roll(base, 2, axis=2)
    return jnp.clip(colored, -40.0, 40.0).astype(jnp.bfloat16)


def plant(entries, rng, smallest, top_value):
    index_at = [jax.random.randint(jax.random.fold_in(rng, axis), (), 0, length) for axis, length in enumerate(entries.shape)]
    main_axis = entries.shape.index(max(entries.shape))
    neighbour = index_at[:main_axis] + [(index_at[main_axis] + 1) % entries.shape[main_axis]] + index_at[main_axis + 1:]
    return entries.at[tuple(index_at)].set(smallest).at[tuple(neighbour)].set(top_value)


def setup_inputs(seed: int = 0, part: int = 0) -> dict:
    keys = jax.random.split(jax.random.key(seed), 3)
    part_splits = jax.random.split(jax.random.fold_in(keys[2], part), 3)
    records = draw_records(jax.random.fold_in(jax.random.fold_in(keys[2], part), 71), part)
    flags = plant((jax.random.randint(part_splits[1], (CHANNELS, SEGS), 0, 4) < 3).astype(jnp.int32), jax.random.fold_in(part_splits[1], 1), 0, 1)
    return {"records": records, "flags": flags}


def lag_tables():
    freq = jnp.arange(BINS, dtype=jnp.int32)
    offset = jnp.arange(LAGS, dtype=jnp.int32) - LAGS // 2
    phase = jnp.mod(freq[:, None] * offset[None, :], SEG_LEN).astype(jnp.float32)
    angle = 2.0 * math.pi * phase / SEG_LEN
    table = jnp.stack([jnp.cos(angle), -jnp.sin(angle)]).astype(jnp.bfloat16)
    return table.astype(jnp.float32)

def reference(records, flags):
    spectra = jnp.fft.rfft(records.astype(jnp.float32), axis=-1)[..., :BINS]
    real_part = jnp.real(spectra).astype(jnp.float32)
    imag_part = jnp.imag(spectra).astype(jnp.float32)
    power = real_part * real_part + imag_part * imag_part
    level = lax.optimization_barrier(jnp.mean(power, axis=-1, keepdims=True))
    valid = flags.astype(jnp.float32)
    scale = valid[..., None] / jnp.sqrt(power + level + 1e-06)
    white = jnp.stack([real_part * scale, imag_part * scale], axis=1).astype(jnp.bfloat16)
    table = lag_tables()
    half = BINS // N_SUB

    def one_block(index):
        first = (index * BLOCK).astype(jnp.int32)
        rows = lax.dynamic_slice_in_dim(white, first, BLOCK, 0).astype(jnp.float32)
        row_flags = lax.dynamic_slice_in_dim(valid, first, BLOCK, 0)
        stacked = jnp.stack([rows.reshape(BLOCK, 2 * SEGS, BINS), jnp.concatenate([rows[:, 1], -rows[:, 0]], axis=1)])
        results = []
        for step in range(STEPS):
            start = (jnp.mod(index - step, N_BLK) * BLOCK).astype(jnp.int32)
            other = lax.dynamic_slice_in_dim(white, start, BLOCK, 0).astype(jnp.float32)
            other = other.reshape(BLOCK, 2 * SEGS, BINS)
            other_flags = lax.dynamic_slice_in_dim(valid, start, BLOCK, 0)
            cross = jnp.einsum('cisf,jsf->cijf', stacked, other, precision=lax.Precision.HIGHEST)
            cross = lax.optimization_barrier(cross.astype(jnp.bfloat16)).astype(jnp.float32)
            total = jnp.zeros((LAGS, BLOCK, BLOCK), jnp.float32)
            for part in range(N_SUB):
                term = jnp.einsum('cfl,cijf->lij', table[:, part * half:(part + 1) * half], cross[..., part * half:(part + 1) * half], precision=lax.Precision.HIGHEST)
                term = lax.optimization_barrier(term.astype(jnp.bfloat16))
                total = total + term.astype(jnp.float32)
            count = jnp.dot(row_flags, other_flags.T, precision=lax.Precision.HIGHEST)
            norm = jnp.sqrt(BINS * jnp.maximum(count, 1.0))
            results.append((total / norm[None]).astype(jnp.bfloat16))
        return jnp.stack(results)
    blocks = lax.map(one_block, jnp.arange(N_BLK, dtype=jnp.int32))
    return blocks.transpose(2, 0, 3, 1, 4).reshape(LAGS, CHANNELS, STEPS, BLOCK)
```

```python
import functools

import jax
import jax.numpy as jnp
import ml_dtypes
import numpy as np
from jax import lax
from jax.experimental import pallas as pl
from jax.experimental.pallas import tpu as pltpu
from jax.sharding import PartitionSpec as P

LAGS = 256
STEPS = 3
LANES = 128
GROUP = 16
PIECES = 2
MESH = pl.DeviceIdType.MESH


def dft_tables(length):
    bins = length // 2
    phase = np.mod(np.arange(length)[:, None] * np.arange(bins)[None, :], length)
    angle = 2.0 * np.pi * phase / length
    return np.cos(angle).astype(np.float32), (-np.sin(angle)).astype(np.float32)


def lag_tables(length):
    bins = length // 2
    phase = np.mod((np.arange(LAGS) - LAGS // 2)[:, None] * np.arange(bins)[None, :], length)
    angle = 2.0 * np.pi * phase / length
    both = np.stack([np.cos(angle), -np.sin(angle)], axis=1).astype(np.float32)
    return both.astype(ml_dtypes.bfloat16)


def regroup_table(segs):
    per = LANES // GROUP
    table = np.zeros((segs, per, GROUP, per, segs, GROUP), np.float32)
    for s in range(segs):
        for q in range(per):
            for f in range(GROUP):
                table[s, q, f, q, s, f] = 1.0
    size = segs * LANES
    return table.reshape(size, size).astype(ml_dtypes.bfloat16)


def row_table(channels, segs):
    table = np.zeros((segs, channels, channels, segs), np.float32)
    for s in range(segs):
        for c in range(channels):
            table[s, c, c, s] = 1.0
    size = segs * channels
    return table.reshape(size, size).astype(ml_dtypes.bfloat16)


def mm(a, b):
    return jnp.dot(a, b, preferred_element_type=jnp.float32)


def mm_t(a, b):
    return lax.dot_general(a, b, (((1,), (1,)), ((), ())), preferred_element_type=jnp.float32)


def kernel(
    blks, grps, dims, normalise,
    rec_ref, flag_ref, row_ref, hi_hbm, lo_hbm, perm_hbm, lag_hbm,
    out_ref, count_ref,
    hi_ref, lo_ref, perm_ref, lag_ref, load_sem, buf, diag, cross, inv, wide, stage, recv_sem, hop_sem, peer_sem, sib_sem,
):
    channels, segs, bins, half = dims
    width = half * 2 * segs
    chunks = half // GROUP
    pair = channels // 2
    loads = [
        pltpu.make_async_copy(source, target, load_sem.at[n])
        for n, (source, target) in enumerate(
            ((hi_hbm, hi_ref), (lo_hbm, lo_ref), (perm_hbm, perm_ref), (lag_hbm, lag_ref)))
    ]
    for load in loads:
        load.start()
    b = lax.axis_index("blk")
    g = lax.axis_index("grp")
    sib = g + 1 - 2 * lax.rem(g, 2)
    core = lax.rem(g, 2)
    across = g + 2 - 4 * lax.rem(g // 2, 2)
    along = g + 4 - 8 * lax.rem(g // 4, 2)
    source = (1 - core) * across + core * along
    target = core * across + (1 - core) * along
    corner = across + along - g
    held = (g, source, target, corner)

    barrier = pltpu.get_barrier_semaphore()
    for k in range(1, STEPS):
        pl.semaphore_signal(barrier, inc=1, device_id={"blk": lax.rem(b + blks - k, blks)}, device_id_type=MESH)
    for other in (across, along, sib):
        pl.semaphore_signal(barrier, inc=1, device_id={"grp": other}, device_id_type=MESH)

    rec = mm(row_ref[...], rec_ref[...]).astype(jnp.bfloat16)
    loads[0].wait()
    spec = mm(rec, hi_ref[...])
    loads[1].wait()
    spec = spec + mm(rec, lo_ref[...])
    real = spec[:, :bins]
    imag = spec[:, bins:]
    power = real * real + imag * imag
    level = jnp.sum(power, axis=1, keepdims=True) / bins
    scale = 1.0 / jnp.sqrt(power[:, :half] + level + 1e-06)
    wide[...] = jnp.zeros_like(wide)
    unit = (lax.broadcasted_iota(jnp.int32, (channels, channels), 0)
            == lax.broadcasted_iota(jnp.int32, (channels, channels), 1)).astype(jnp.float32)
    wide[:, :segs] = mm_t(unit, flag_ref[...].astype(jnp.float32))
    flags = wide[...]
    pieces = [(real[:, :half] * scale).astype(jnp.bfloat16), (imag[:, :half] * scale).astype(jnp.bfloat16)]
    rows = []
    for t in range(half // LANES):
        for piece in pieces:
            rows.append(jnp.concatenate([
                piece[s * channels:(s + 1) * channels, t * LANES:(t + 1) * LANES]
                * flags[:, s:s + 1].astype(jnp.bfloat16)
                for s in range(segs)
            ], axis=1))
    loads[2].wait()
    regrouped = mm(jnp.concatenate(rows, axis=0), perm_ref[...]).astype(jnp.bfloat16)
    per = LANES // GROUP
    for t in range(half // LANES):
        for i in range(2):
            part = regrouped[(t * 2 + i) * channels:(t * 2 + i + 1) * channels]
            for q in range(per):
                at = ((t * per + q) * 2 + i) * LANES
                buf[0, g, :, at:at + LANES] = part[:, q * LANES:(q + 1) * LANES]
    buf[0, g, :, width:width + LANES] = flags.astype(jnp.bfloat16)

    pl.semaphore_wait(barrier, STEPS - 1 + 3)

    sent = []

    cut = width // PIECES
    spans = [(h * cut, cut if h < PIECES - 1 else width + LANES - h * cut) for h in range(PIECES)]
    steps = [(k, h) for k in range(STEPS) for h in range(PIECES)]

    def piece(k, h, slot):
        return buf.at[k, slot, :, pl.ds(*spans[h])]

    def send(source, target, send_sem, landed, where):
        copy = pltpu.make_async_remote_copy(
            src_ref=source, dst_ref=target, send_sem=send_sem, recv_sem=landed,
            device_id=where, device_id_type=MESH,
        )
        copy.start()
        sent.append(copy)

    def arrived(k, h, slot):
        ref = piece(k, h, slot)
        pltpu.make_async_copy(ref, ref, recv_sem.at[k, h, slot]).wait()

    def give(k, h, slot, n, other, sem):
        ref = piece(k, h, slot)
        send(ref, ref, sem.at[k, h, n], recv_sem.at[k, h, slot], {"grp": other})

    def spread(n):
        if n < len(steps):
            k, h = steps[n]
            if k:
                arrived(k, h, g)
            give(k, h, g, 0, target, peer_sem)
            give(k, h, g, 1, source, peer_sem)
            give(k, h, g, 0, sib, sib_sem)

    def forward(n):
        if n < len(steps):
            k, h = steps[n]
            arrived(k, h, source)
            give(k, h, source, 2, target, peer_sem)
            give(k, h, source, 1, sib, sib_sem)
            arrived(k, h, target)
            give(k, h, target, 2, sib, sib_sem)

    def finish(n):
        if n < len(steps):
            k, h = steps[n]
            arrived(k, h, corner)
            give(k, h, corner, 3, sib, sib_sem)

    def gather(n):
        k, h = steps[n]
        for slot in held:
            arrived(k, h, slot + 1 - 2 * lax.rem(slot, 2))

    def hop(h):
        for k in range(1, STEPS):
            send(piece(0, h, g), piece(k, h, g), hop_sem.at[k, h], recv_sem.at[k, h, g],
                 {"blk": lax.rem(b + k, blks)})

    for h in range(PIECES):
        spread(h)
        hop(h)

    size = 2 * segs * GROUP
    same = (lax.broadcasted_iota(jnp.int32, (channels * GROUP, size), 0) % GROUP
            == lax.broadcasted_iota(jnp.int32, (channels * GROUP, size), 1) % GROUP)

    def build(q, carry):
        at = pl.multiple_of(q * size, size)
        first = buf[0, g, :, pl.ds(at, size)].astype(jnp.float32)
        second = jnp.concatenate([first[:, LANES:], -first[:, :LANES]], axis=1)
        for i, value in enumerate((first, second)):
            wide = jnp.broadcast_to(value[:, None, :], (channels, GROUP, size)).reshape(channels * GROUP, size)
            diag[q, i * channels * GROUP:(i + 1) * channels * GROUP, :] = jnp.where(same, wide, 0.0).astype(jnp.bfloat16)
        return carry

    lax.fori_loop(0, chunks // 2, build, 0)
    forward(0)
    spread(PIECES)
    lax.fori_loop(chunks // 2, chunks, build, 0)
    forward(1)
    finish(0)
    spread(PIECES + 1)
    loads[3].wait()
    block = grps * channels
    unroll = 4

    def multiply(group, carry, k):
        for u in range(unroll):
            q = group * unroll + u
            at = pl.multiple_of(q * size, size)
            other = buf[k, :, :, pl.ds(at, size)].reshape(block, size)
            product = mm_t(diag[q], other).astype(jnp.bfloat16).reshape(2, 2, pair, GROUP, block)
            low = pl.multiple_of(q * GROUP, GROUP)
            for i in range(2):
                for p in range(2):
                    cross[:, i, pl.ds(low, GROUP), p * block:(p + 1) * block] = product[i, p]
        return carry

    def lag(c, carry, k):
        total = mm(lag_ref[...], cross[c].reshape(2 * half, 2 * block)).astype(jnp.bfloat16)
        if normalise:
            total = (total.astype(jnp.float32) * inv[pl.ds(c, 1), :]).astype(jnp.bfloat16)
        total = total.astype(jnp.float32)
        stage[pl.ds(c, LAGS, stride=channels), :] = total[:, :block]
        stage[pl.ds(c + pair, LAGS, stride=channels), :] = total[:, block:]
        return carry

    def place(n, carry, k):
        low = pl.multiple_of(n * 16, 16)
        part = stage[pl.ds(pl.multiple_of(n * 16 * channels, 16), 16 * channels), :]
        out_ref[pl.ds(low, 16), k] = part.astype(jnp.bfloat16).reshape(16, channels, block)
        return carry

    groups = chunks // PIECES // unroll
    for n, (k, h) in enumerate(steps):
        forward(n + 2)
        finish(n + 1)
        if n + PIECES + 2 < len(steps):
            spread(n + PIECES + 2)
        gather(n)
        lax.fori_loop(h * groups, (h + 1) * groups, functools.partial(multiply, k=k), 0)
        if h == PIECES - 1:
            tile = buf[k, :, :, width:width + LANES].reshape(block, LANES)
            count = mm_t(flags.astype(jnp.bfloat16), tile)
            count_ref[:, k * block:(k + 1) * block] = count
            factor = lax.rsqrt(bins * jnp.maximum(count, 1.0))
            inv[:, :block] = factor[:pair]
            inv[:, block:] = factor[pair:]
            lax.fori_loop(0, pair, functools.partial(lag, k=k), 0)
            lax.fori_loop(0, LAGS // 16, functools.partial(place, k=k), 0)

    for copy in sent:
        copy.wait_send()


def on_device(records, flags):
    channels, segs, length = records.shape
    bins = length // 2
    splits = lax.axis_size("sub")
    blks = lax.axis_size("blk")
    grps = lax.axis_size("grp")
    half = bins // splits
    block = grps * channels
    cos, sin = dft_tables(length)
    lags = lag_tables(length)
    both = np.stack([cos, sin], axis=1)
    high = both.astype(ml_dtypes.bfloat16)
    low = (both - high.astype(np.float32)).astype(ml_dtypes.bfloat16)
    high, low, lags = jnp.asarray(high), jnp.asarray(low), jnp.asarray(lags)
    if splits > 1:
        first = lax.axis_index("sub") * half
        high = jnp.roll(high, -first, axis=2)
        low = jnp.roll(low, -first, axis=2)
        lags = lax.dynamic_slice_in_dim(lags, first, half, 2)
    width = half * 2 * segs + LANES
    vmem = pl.BlockSpec(memory_space=pltpu.VMEM)
    out, count = pl.pallas_call(
        functools.partial(kernel, blks, grps, (channels, segs, bins, half), splits == 1),
        out_shape=(
            pltpu.VMEM((LAGS, STEPS, channels, block), jnp.bfloat16),
            jax.ShapeDtypeStruct((channels, STEPS * block), jnp.float32),
        ),
        in_specs=[vmem] * 3 + [pl.BlockSpec(memory_space=pltpu.HBM)] * 4,
        out_specs=(vmem, vmem),
        scratch_shapes=[
            pltpu.VMEM((length, 2 * bins), jnp.bfloat16),
            pltpu.VMEM((length, 2 * bins), jnp.bfloat16),
            pltpu.VMEM((segs * LANES, segs * LANES), jnp.bfloat16),
            pltpu.VMEM((LAGS, 2 * half), jnp.bfloat16),
            pltpu.SemaphoreType.DMA((4,)),
            pltpu.VMEM((STEPS, grps, channels, width), jnp.bfloat16),
            pltpu.VMEM((half // GROUP, 2 * channels * GROUP, 2 * segs * GROUP), jnp.bfloat16),
            pltpu.VMEM((channels // 2, 2, half, 2 * block), jnp.bfloat16),
            pltpu.VMEM((channels // 2, 2 * block), jnp.float32),
            pltpu.VMEM((channels, LANES), jnp.float32),
            pltpu.VMEM(((LAGS + 1) * channels, block), jnp.float32),
            pltpu.SemaphoreType.DMA((STEPS, PIECES, grps)),
            pltpu.SemaphoreType.DMA((STEPS, PIECES)),
            pltpu.SemaphoreType.DMA((STEPS, PIECES, 3)),
            pltpu.SemaphoreType.DMA((STEPS, PIECES, grps // 2)),
        ],
        compiler_params=pltpu.CompilerParams(
            collective_id=0, has_side_effects=True, vmem_limit_bytes=52 * 1024 * 1024
        ),
    )(
        records.reshape(channels * segs, length),
        flags.T,
        jnp.asarray(row_table(channels, segs)),
        high.reshape(length, 2 * bins),
        low.reshape(length, 2 * bins),
        jnp.asarray(regroup_table(segs)),
        lags.reshape(LAGS, 2 * half),
    )
    out = out.transpose(0, 2, 1, 3)
    if splits > 1:
        out = lax.psum_scatter(out, "sub", scatter_dimension=0, tiled=True).astype(jnp.float32)
        out = (out / jnp.sqrt(bins * jnp.maximum(count, 1.0)).reshape(1, channels, STEPS, block)).astype(jnp.bfloat16)
    return out


def solution(mesh):
    return jax.shard_map(
        on_device,
        mesh=mesh,
        in_specs=(P(("dom", "blk", "grp"), None, None), P(("dom", "blk", "grp"), None)),
        out_specs=P("sub", ("dom", "blk", "grp"), None, None),
        check_vma=False,
    )
```

```python
import functools

import jax
import jax.numpy as jnp
import ml_dtypes
import numpy as np
from jax import lax
from jax.experimental import pallas as pl
from jax.experimental.pallas import tpu as pltpu
from jax.sharding import PartitionSpec as P

LAGS = 256
STEPS = 3
LANES = 128
GROUP = 16
PIECES = 2
MESH = pl.DeviceIdType.MESH


def dft_tables(length):
    bins = length // 2
    phase = np.mod(np.arange(length)[:, None] * np.arange(bins)[None, :], length)
    angle = 2.0 * np.pi * phase / length
    return np.cos(angle).astype(np.float32), (-np.sin(angle)).astype(np.float32)


def lag_tables(length):
    bins = length // 2
    phase = np.mod((np.arange(LAGS) - LAGS // 2)[:, None] * np.arange(bins)[None, :], length)
    angle = 2.0 * np.pi * phase / length
    both = np.stack([np.cos(angle), -np.sin(angle)], axis=1).astype(np.float32)
    return both.astype(ml_dtypes.bfloat16)


def regroup_table(segs):
    per = LANES // GROUP
    table = np.zeros((segs, per, GROUP, per, segs, GROUP), np.float32)
    for s in range(segs):
        for q in range(per):
            for f in range(GROUP):
                table[s, q, f, q, s, f] = 1.0
    size = segs * LANES
    return table.reshape(size, size).astype(ml_dtypes.bfloat16)


def row_table(channels, segs):
    table = np.zeros((segs, channels, channels, segs), np.float32)
    for s in range(segs):
        for c in range(channels):
            table[s, c, c, s] = 1.0
    size = segs * channels
    return table.reshape(size, size).astype(ml_dtypes.bfloat16)


def mm(a, b):
    return jnp.dot(a, b, preferred_element_type=jnp.float32)


def mm_t(a, b):
    return lax.dot_general(a, b, (((1,), (1,)), ((), ())), preferred_element_type=jnp.float32)


def kernel(
    blks, grps, dims, normalise,
    rec_ref, flag_ref, row_ref, hi_hbm, lo_hbm, perm_hbm, lag_hbm,
    out_ref, count_ref,
    hi_ref, lo_ref, perm_ref, lag_ref, load_sem, buf, diag, cross, inv, wide, stage, recv_sem, hop_sem, peer_sem, sib_sem,
):
    channels, segs, bins, half = dims
    width = half * 2 * segs
    chunks = half // GROUP
    pair = channels // 2
    loads = [
        pltpu.make_async_copy(source, target, load_sem.at[n])
        for n, (source, target) in enumerate(
            ((hi_hbm, hi_ref), (lo_hbm, lo_ref), (perm_hbm, perm_ref), (lag_hbm, lag_ref)))
    ]
    for load in loads:
        load.start()
    b = lax.axis_index("blk")
    g = lax.axis_index("grp")
    sib = g + 1 - 2 * lax.rem(g, 2)
    core = lax.rem(g, 2)
    across = g + 2 - 4 * lax.rem(g // 2, 2)
    along = g + 4 - 8 * lax.rem(g // 4, 2)
    source = (1 - core) * across + core * along
    target = core * across + (1 - core) * along
    corner = across + along - g
    held = (g, source, target, corner)

    barrier = pltpu.get_barrier_semaphore()
    for k in range(1, STEPS):
        pl.semaphore_signal(barrier, inc=1, device_id={"blk": lax.rem(b + blks - k, blks)}, device_id_type=MESH)
    for other in (across, along, sib):
        pl.semaphore_signal(barrier, inc=1, device_id={"grp": other}, device_id_type=MESH)

    rec = mm(row_ref[...], rec_ref[...]).astype(jnp.bfloat16)
    loads[0].wait()
    spec = mm(rec, hi_ref[...])
    loads[1].wait()
    spec = spec + mm(rec, lo_ref[...])
    real = spec[:, :bins]
    imag = spec[:, bins:]
    power = real * real + imag * imag
    level = jnp.sum(power, axis=1, keepdims=True) / bins
    scale = 1.0 / jnp.sqrt(power[:, :half] + level + 1e-06)
    wide[...] = jnp.zeros_like(wide)
    unit = (lax.broadcasted_iota(jnp.int32, (channels, channels), 0)
            == lax.broadcasted_iota(jnp.int32, (channels, channels), 1)).astype(jnp.float32)
    wide[:, :segs] = mm_t(unit, flag_ref[...].astype(jnp.float32))
    flags = wide[...]
    pieces = [(real[:, :half] * scale).astype(jnp.bfloat16), (imag[:, :half] * scale).astype(jnp.bfloat16)]
    rows = []
    for t in range(half // LANES):
        for piece in pieces:
            rows.append(jnp.concatenate([
                piece[s * channels:(s + 1) * channels, t * LANES:(t + 1) * LANES]
                * flags[:, s:s + 1].astype(jnp.bfloat16)
                for s in range(segs)
            ], axis=1))
    loads[2].wait()
    regrouped = mm(jnp.concatenate(rows, axis=0), perm_ref[...]).astype(jnp.bfloat16)
    per = LANES // GROUP
    for t in range(half // LANES):
        for i in range(2):
            part = regrouped[(t * 2 + i) * channels:(t * 2 + i + 1) * channels]
            for q in range(per):
                at = ((t * per + q) * 2 + i) * LANES
                buf[0, g, :, at:at + LANES] = part[:, q * LANES:(q + 1) * LANES]
    buf[0, g, :, width:width + LANES] = flags.astype(jnp.bfloat16)

    pl.semaphore_wait(barrier, STEPS - 1 + 3)

    sent = []

    cut = width // PIECES
    spans = [(h * cut, cut if h < PIECES - 1 else width + LANES - h * cut) for h in range(PIECES)]
    steps = [(k, h) for k in range(STEPS) for h in range(PIECES)]

    def piece(k, h, slot):
        return buf.at[k, slot, :, pl.ds(*spans[h])]

    def send(source, target, send_sem, landed, where):
        copy = pltpu.make_async_remote_copy(
            src_ref=source, dst_ref=target, send_sem=send_sem, recv_sem=landed,
            device_id=where, device_id_type=MESH,
        )
        copy.start()
        sent.append(copy)

    def arrived(k, h, slot):
        ref = piece(k, h, slot)
        pltpu.make_async_copy(ref, ref, recv_sem.at[k, h, slot]).wait()

    def give(k, h, slot, n, other, sem):
        ref = piece(k, h, slot)
        send(ref, ref, sem.at[k, h, n], recv_sem.at[k, h, slot], {"grp": other})

    def spread(n):
        if n < len(steps):
            k, h = steps[n]
            if k:
                arrived(k, h, g)
            give(k, h, g, 0, target, peer_sem)
            give(k, h, g, 1, source, peer_sem)
            give(k, h, g, 0, sib, sib_sem)

    def forward(n):
        if n < len(steps):
            k, h = steps[n]
            arrived(k, h, source)
            give(k, h, source, 2, target, peer_sem)
            give(k, h, source, 1, sib, sib_sem)
            arrived(k, h, target)
            give(k, h, target, 2, sib, sib_sem)

    def finish(n):
        if n < len(steps):
            k, h = steps[n]
            arrived(k, h, corner)
            give(k, h, corner, 3, sib, sib_sem)

    def gather(n):
        k, h = steps[n]
        for slot in held:
            arrived(k, h, slot + 1 - 2 * lax.rem(slot, 2))

    def hop(h):
        for k in range(1, STEPS):
            send(piece(0, h, g), piece(k, h, g), hop_sem.at[k, h], recv_sem.at[k, h, g],
                 {"blk": lax.rem(b + k, blks)})

    for h in range(PIECES):
        spread(h)
        hop(h)

    size = 2 * segs * GROUP
    few = GROUP // 2
    same = (lax.broadcasted_iota(jnp.int32, (channels * few, size), 0) % few
            == lax.broadcasted_iota(jnp.int32, (channels * few, size), 1) % few)

    def build(q, carry):
        at = pl.multiple_of(q * size, size)
        first = buf[0, g, :, pl.ds(at, size)].astype(jnp.float32)
        second = jnp.concatenate([first[:, LANES:], -first[:, :LANES]], axis=1)
        for i, value in enumerate((first, second)):
            wide = jnp.broadcast_to(value[:, None, :], (channels, few, size)).reshape(channels * few, size)
            diag[q, i * channels * few:(i + 1) * channels * few, :] = jnp.where(same, wide, 0.0).astype(jnp.bfloat16)
        return carry

    lax.fori_loop(0, chunks // 2, build, 0)
    forward(0)
    spread(PIECES)
    lax.fori_loop(chunks // 2, chunks, build, 0)
    forward(1)
    finish(0)
    spread(PIECES + 1)
    loads[3].wait()
    block = grps * channels
    unroll = min(16, chunks // PIECES)
    upper = lax.broadcasted_iota(jnp.int32, (block, size), 1) % GROUP >= few

    def multiply(group, carry, k):
        for u in range(unroll):
            q = group * unroll + u
            at = pl.multiple_of(q * size, size)
            other = buf[k, :, :, pl.ds(at, size)].reshape(block, size)
            zero = jnp.zeros_like(other)
            other = jnp.concatenate([jnp.where(upper, zero, other), jnp.where(upper, other, zero)], axis=0)
            product = mm_t(diag[q], other).reshape(2, 2, pair, few, 2 * block)
            product = jnp.concatenate([product[..., :block], product[..., block:]], axis=3).astype(jnp.bfloat16)
            low = pl.multiple_of(q * GROUP, GROUP)
            for i in range(2):
                for p in range(2):
                    cross[:, i, pl.ds(low, GROUP), p * block:(p + 1) * block] = product[i, p]
        return carry

    def lag(c, carry, k):
        total = mm(lag_ref[...], cross[c].reshape(2 * half, 2 * block)).astype(jnp.bfloat16)
        if normalise:
            total = (total.astype(jnp.float32) * inv[pl.ds(c, 1), :]).astype(jnp.bfloat16)
        total = total.astype(jnp.float32)
        stage[pl.ds(c, LAGS, stride=channels), :] = total[:, :block]
        stage[pl.ds(c + pair, LAGS, stride=channels), :] = total[:, block:]
        return carry

    def place(n, carry, k):
        low = pl.multiple_of(n * 16, 16)
        part = stage[pl.ds(pl.multiple_of(n * 16 * channels, 16), 16 * channels), :]
        out_ref[pl.ds(low, 16), k] = part.astype(jnp.bfloat16).reshape(16, channels, block)
        return carry

    groups = chunks // PIECES // unroll
    for n, (k, h) in enumerate(steps):
        forward(n + 2)
        finish(n + 1)
        if n + PIECES + 2 < len(steps):
            spread(n + PIECES + 2)
        gather(n)
        lax.fori_loop(h * groups, (h + 1) * groups, functools.partial(multiply, k=k), 0)
        if h == PIECES - 1:
            tile = buf[k, :, :, width:width + LANES].reshape(block, LANES)
            count = mm_t(flags.astype(jnp.bfloat16), tile)
            count_ref[:, k * block:(k + 1) * block] = count
            factor = lax.rsqrt(bins * jnp.maximum(count, 1.0))
            inv[:, :block] = factor[:pair]
            inv[:, block:] = factor[pair:]
            lax.fori_loop(0, pair, functools.partial(lag, k=k), 0, unroll=4)
            lax.fori_loop(0, LAGS // 16, functools.partial(place, k=k), 0, unroll=4)

    for copy in sent:
        copy.wait_send()


def on_device(records, flags):
    channels, segs, length = records.shape
    bins = length // 2
    splits = lax.axis_size("sub")
    blks = lax.axis_size("blk")
    grps = lax.axis_size("grp")
    half = bins // splits
    block = grps * channels
    cos, sin = dft_tables(length)
    lags = lag_tables(length)
    both = np.stack([cos, sin], axis=1)
    high = both.astype(ml_dtypes.bfloat16)
    low = (both - high.astype(np.float32)).astype(ml_dtypes.bfloat16)
    high, low, lags = jnp.asarray(high), jnp.asarray(low), jnp.asarray(lags)
    if splits > 1:
        first = lax.axis_index("sub") * half
        high = jnp.roll(high, -first, axis=2)
        low = jnp.roll(low, -first, axis=2)
        lags = lax.dynamic_slice_in_dim(lags, first, half, 2)
    width = half * 2 * segs + LANES
    vmem = pl.BlockSpec(memory_space=pltpu.VMEM)
    out, count = pl.pallas_call(
        functools.partial(kernel, blks, grps, (channels, segs, bins, half), splits == 1),
        out_shape=(
            pltpu.VMEM((LAGS, STEPS, channels, block), jnp.bfloat16),
            jax.ShapeDtypeStruct((channels, STEPS * block), jnp.float32),
        ),
        in_specs=[vmem] * 3 + [pl.BlockSpec(memory_space=pltpu.HBM)] * 4,
        out_specs=(vmem, vmem),
        scratch_shapes=[
            pltpu.VMEM((length, 2 * bins), jnp.bfloat16),
            pltpu.VMEM((length, 2 * bins), jnp.bfloat16),
            pltpu.VMEM((segs * LANES, segs * LANES), jnp.bfloat16),
            pltpu.VMEM((LAGS, 2 * half), jnp.bfloat16),
            pltpu.SemaphoreType.DMA((4,)),
            pltpu.VMEM((STEPS, grps, channels, width), jnp.bfloat16),
            pltpu.VMEM((half // GROUP, channels * GROUP, 2 * segs * GROUP), jnp.bfloat16),
            pltpu.VMEM((channels // 2, 2, half, 2 * block), jnp.bfloat16),
            pltpu.VMEM((channels // 2, 2 * block), jnp.float32),
            pltpu.VMEM((channels, LANES), jnp.float32),
            pltpu.VMEM(((LAGS + 1) * channels, block), jnp.float32),
            pltpu.SemaphoreType.DMA((STEPS, PIECES, grps)),
            pltpu.SemaphoreType.DMA((STEPS, PIECES)),
            pltpu.SemaphoreType.DMA((STEPS, PIECES, 3)),
            pltpu.SemaphoreType.DMA((STEPS, PIECES, grps // 2)),
        ],
        compiler_params=pltpu.CompilerParams(
            collective_id=0, has_side_effects=True, vmem_limit_bytes=52 * 1024 * 1024
        ),
    )(
        records.reshape(channels * segs, length),
        flags.T,
        jnp.asarray(row_table(channels, segs)),
        high.reshape(length, 2 * bins),
        low.reshape(length, 2 * bins),
        jnp.asarray(regroup_table(segs)),
        lags.reshape(LAGS, 2 * half),
    )
    out = out.transpose(0, 2, 1, 3)
    if splits > 1:
        out = lax.psum_scatter(out, "sub", scatter_dimension=0, tiled=True).astype(jnp.float32)
        out = (out / jnp.sqrt(bins * jnp.maximum(count, 1.0)).reshape(1, channels, STEPS, block)).astype(jnp.bfloat16)
    return out


def solution(mesh):
    return jax.shard_map(
        on_device,
        mesh=mesh,
        in_specs=(P(("dom", "blk", "grp"), None, None), P(("dom", "blk", "grp"), None)),
        out_specs=P("sub", ("dom", "blk", "grp"), None, None),
        check_vma=False,
    )
```

```python
import functools

import jax
import jax.numpy as jnp
import ml_dtypes
import numpy as np
from jax import lax
from jax.experimental import pallas as pl
from jax.experimental.pallas import tpu as pltpu
from jax.sharding import PartitionSpec as P

LAGS = 256
STEPS = 3
LANES = 128
GROUP = 16
SPLIT = (0, 1, 2)
PIECES = len(SPLIT) - 1
CLIMB = ((1, 0), (1, 1), (2, 1))
ORDER = (
    ("s", 0), ("s", 1), ("f", 0), ("t", 0), ("b", 0), ("s", 2), ("f", 1), ("s", 3), ("c", 0), ("m", 0), ("s", 4), ("t", 1), ("f", 2), ("c", 1), ("t", 2), ("s", 5), ("b", 1), ("c", 2), ("m", 1), ("t", 3), ("f", 3), ("e", 0), ("c", 3), ("f", 4), ("m", 2), ("t", 4), ("t", 5), ("f", 5), ("m", 3), ("c", 4), ("e", 1), ("c", 5), ("m", 4), ("m", 5), ("e", 2),
)
MESH = pl.DeviceIdType.MESH


def dft_tables(length):
    bins = length // 2
    phase = np.mod(np.arange(length)[:, None] * np.arange(bins)[None, :], length)
    angle = 2.0 * np.pi * phase / length
    return np.cos(angle).astype(np.float32), (-np.sin(angle)).astype(np.float32)


def lag_tables(length):
    bins = length // 2
    phase = np.mod((np.arange(LAGS) - LAGS // 2)[:, None] * np.arange(bins)[None, :], length)
    angle = 2.0 * np.pi * phase / length
    both = np.stack([np.cos(angle), -np.sin(angle)], axis=1).astype(np.float32)
    return both.astype(ml_dtypes.bfloat16)


def row_table(channels, segs):
    table = np.zeros((segs, channels, channels, segs), np.float32)
    for s in range(segs):
        for c in range(channels):
            table[s, c, c, s] = 1.0
    size = segs * channels
    return table.reshape(size, size).astype(ml_dtypes.bfloat16)


def mm(a, b):
    return jnp.dot(a, b, preferred_element_type=jnp.float32)


def mm_t(a, b):
    return lax.dot_general(a, b, (((1,), (1,)), ((), ())), preferred_element_type=jnp.float32)


def kernel(
    blks, grps, dims, normalise,
    rec_ref, flag_ref, row_ref, hi_hbm, lag_hbm,
    out_ref, count_ref,
    hi_ref, perm_ref, lag_ref, load_sem, buf, diag, cross, inv, wide, stage, recv_sem, hop_sem, peer_sem, sib_sem,
):
    channels, segs, bins, half = dims
    width = half * 2 * segs
    chunks = half // GROUP
    pair = channels // 2
    loads = [
        pltpu.make_async_copy(source, target, load_sem.at[n])
        for n, (source, target) in enumerate(
            ((hi_hbm, hi_ref), (lag_hbm, lag_ref)))
    ]
    for load in loads[:-1]:
        load.start()
    b = lax.axis_index("blk")
    g = lax.axis_index("grp")
    sib = g + 1 - 2 * lax.rem(g, 2)
    core = lax.rem(g, 2)
    across = g + 2 - 4 * lax.rem(g // 2, 2)
    along = g + 4 - 8 * lax.rem(g // 4, 2)
    source = (1 - core) * across + core * along
    target = core * across + (1 - core) * along
    corner = across + along - g
    held = (g, source, target, corner)

    barrier = pltpu.get_barrier_semaphore()
    pl.semaphore_signal(barrier, inc=1, device_id={"blk": lax.rem(b + blks - 1, blks)}, device_id_type=MESH)
    for other in (across, along, sib):
        pl.semaphore_signal(barrier, inc=1, device_id={"grp": other}, device_id_type=MESH)

    per = LANES // GROUP
    came = lax.broadcasted_iota(jnp.int32, (segs * LANES, 1), 0)
    goes = came // GROUP % per * LANES + came // LANES * GROUP + came % GROUP
    lane = lax.broadcasted_iota(jnp.int32, (segs * LANES, LANES), 1)
    for q in range(per):
        perm_ref[:, q * LANES:(q + 1) * LANES] = jnp.where(goes == lane + q * LANES, 1.0, 0.0).astype(jnp.bfloat16)
    rec = mm(row_ref[...], rec_ref[...]).astype(jnp.bfloat16)
    loads[0].wait()
    spec = mm(rec, hi_ref[...])
    real = spec[:, :bins]
    imag = spec[:, bins:]
    power = real * real + imag * imag
    level = jnp.sum(power, axis=1, keepdims=True) / bins
    scale = 1.0 / jnp.sqrt(power[:, :half] + level + 1e-06)
    wide[...] = jnp.zeros_like(wide)
    unit = (lax.broadcasted_iota(jnp.int32, (channels, channels), 0)
            == lax.broadcasted_iota(jnp.int32, (channels, channels), 1)).astype(jnp.float32)
    wide[:, :segs] = mm_t(unit, flag_ref[...].astype(jnp.float32))
    flags = wide[...]
    pieces = [(real[:, :half] * scale).astype(jnp.bfloat16), (imag[:, :half] * scale).astype(jnp.bfloat16)]
    rows = []
    for t in range(half // LANES):
        for piece in pieces:
            rows.append(jnp.concatenate([
                piece[s * channels:(s + 1) * channels, t * LANES:(t + 1) * LANES]
                * flags[:, s:s + 1].astype(jnp.bfloat16)
                for s in range(segs)
            ], axis=1))
    regrouped = mm(jnp.concatenate(rows, axis=0), perm_ref[...]).astype(jnp.bfloat16)
    for t in range(half // LANES):
        for i in range(2):
            part = regrouped[(t * 2 + i) * channels:(t * 2 + i + 1) * channels]
            for q in range(per):
                at = ((t * per + q) * 2 + i) * LANES
                buf[0, g, :, at:at + LANES] = part[:, q * LANES:(q + 1) * LANES]
    buf[0, g, :, width:width + LANES] = flags.astype(jnp.bfloat16)

    loads[-1].start()
    pl.semaphore_wait(barrier, 4)

    sent = []

    bounds = [chunks * part // SPLIT[-1] for part in SPLIT]
    edges = [2 * segs * GROUP * bound for bound in bounds[:-1]] + [width + LANES]
    spans = [(low, high - low) for low, high in zip(edges[:-1], edges[1:])]
    steps = [(k, h) for k in range(STEPS) for h in range(PIECES)]

    def piece(k, h, slot):
        return buf.at[k, slot, :, pl.ds(*spans[h])]

    def send(source, target, send_sem, landed, where):
        copy = pltpu.make_async_remote_copy(
            src_ref=source, dst_ref=target, send_sem=send_sem, recv_sem=landed,
            device_id=where, device_id_type=MESH,
        )
        copy.start()
        sent.append(copy)

    def arrived(k, h, slot):
        ref = piece(k, h, slot)
        pltpu.make_async_copy(ref, ref, recv_sem.at[k, h, slot]).wait()

    def give(k, h, slot, n, other, sem):
        ref = piece(k, h, slot)
        send(ref, ref, sem.at[k, h, n], recv_sem.at[k, h, slot], {"grp": other})

    def rise(k, h, slot, n):
        send(piece(k, h, slot), piece(k + 1, h, slot), hop_sem.at[k, h, n], recv_sem.at[k + 1, h, slot],
             {"blk": lax.rem(b + 1, blks)})

    def spread(n):
        k, h = steps[n]
        if k:
            arrived(k, h, g)
        if k + 1 < STEPS:
            rise(k, h, g, 0)
        give(k, h, g, 0, target, peer_sem)
        give(k, h, g, 1, source, peer_sem)
        give(k, h, g, 0, sib, sib_sem)

    def forward(n):
        k, h = steps[n]
        arrived(k, h, source)
        if (k, h) not in CLIMB:
            give(k, h, source, 2, target, peer_sem)
        give(k, h, source, 1, sib, sib_sem)

    def relay(n):
        k, h = steps[n]
        arrived(k, h, target)
        give(k, h, target, 2, sib, sib_sem)

    def finish(n):
        k, h = steps[n]
        arrived(k, h, corner)
        if (k + 1, h) in CLIMB:
            rise(k, h, corner, 1)
        give(k, h, corner, 3, sib, sib_sem)

    def gather(n):
        k, h = steps[n]
        for slot in held:
            arrived(k, h, slot + 1 - 2 * lax.rem(slot, 2))

    size = 2 * segs * GROUP
    few = GROUP // 2
    same = (lax.broadcasted_iota(jnp.int32, (channels * few, size), 0) % few
            == lax.broadcasted_iota(jnp.int32, (channels * few, size), 1) % few)

    def build(q, carry):
        at = pl.multiple_of(q * size, size)
        first = buf[0, g, :, pl.ds(at, size)].astype(jnp.float32)
        second = jnp.concatenate([first[:, LANES:], -first[:, :LANES]], axis=1)
        for i, value in enumerate((first, second)):
            wide = jnp.broadcast_to(value[:, None, :], (channels, few, size)).reshape(channels * few, size)
            diag[q, i * channels * few:(i + 1) * channels * few, :] = jnp.where(same, wide, 0.0).astype(jnp.bfloat16)
        return carry

    block = grps * channels
    upper = lax.broadcasted_iota(jnp.int32, (block, size), 1) % GROUP >= few

    def multiply(q, k):
        other = buf[k, :, :, q * size:(q + 1) * size].reshape(block, size)
        zero = jnp.zeros_like(other)
        other = jnp.concatenate([jnp.where(upper, zero, other), jnp.where(upper, other, zero)], axis=0)
        product = mm_t(diag[q], other).reshape(2, 2, pair, few, 2 * block)
        product = jnp.concatenate([product[..., :block], product[..., block:]], axis=3).astype(jnp.bfloat16)
        for i in range(2):
            for p in range(2):
                cross[:, i, q * GROUP:(q + 1) * GROUP, p * block:(p + 1) * block] = product[i, p]

    def lag(c, carry, k):
        total = mm(lag_ref[...], cross[c].reshape(2 * half, 2 * block)).astype(jnp.bfloat16)
        if normalise:
            total = (total.astype(jnp.float32) * inv[pl.ds(c, 1), :]).astype(jnp.bfloat16)
        total = total.astype(jnp.float32)
        stage[pl.ds(c, LAGS, stride=channels), :] = total[:, :block]
        stage[pl.ds(c + pair, LAGS, stride=channels), :] = total[:, block:]
        return carry

    def place(n, carry, k):
        low = pl.multiple_of(n * 16, 16)
        part = stage[pl.ds(pl.multiple_of(n * 16 * channels, 16), 16 * channels), :]
        out_ref[pl.ds(low, 16), k] = part.astype(jnp.bfloat16).reshape(16, channels, block)
        return carry

    def prepare(n):
        lax.fori_loop(bounds[n], bounds[n + 1], build, 0, unroll=2)

    def combine(n):
        k, h = steps[n]
        gather(n)
        for q in range(bounds[h], bounds[h + 1]):
            multiply(q, k)

    def emit(k):
        if k == 0:
            loads[-1].wait()
        tile = buf[k, :, :, width:width + LANES].reshape(block, LANES)
        count = mm_t(flags.astype(jnp.bfloat16), tile)
        count_ref[:, k * block:(k + 1) * block] = count
        factor = lax.rsqrt(bins * jnp.maximum(count, 1.0))
        inv[:, :block] = factor[:pair]
        inv[:, block:] = factor[pair:]
        lax.fori_loop(0, pair, functools.partial(lag, k=k), 0, unroll=4)
        lax.fori_loop(0, LAGS // 16, functools.partial(place, k=k), 0, unroll=4)

    acts = {"s": spread, "f": forward, "t": relay, "c": finish, "b": prepare, "m": combine, "e": emit}
    for act, n in ORDER:
        acts[act](n)

    for copy in sent:
        copy.wait_send()


def on_device(records, flags):
    channels, segs, length = records.shape
    bins = length // 2
    splits = lax.axis_size("sub")
    blks = lax.axis_size("blk")
    grps = lax.axis_size("grp")
    half = bins // splits
    block = grps * channels
    cos, sin = dft_tables(length)
    lags = lag_tables(length)
    both = np.stack([cos, sin], axis=1)
    high = both.astype(ml_dtypes.bfloat16)
    high, lags = jnp.asarray(high), jnp.asarray(lags)
    if splits > 1:
        first = lax.axis_index("sub") * half
        high = jnp.roll(high, -first, axis=2)
        lags = lax.dynamic_slice_in_dim(lags, first, half, 2)
    width = half * 2 * segs + LANES
    vmem = pl.BlockSpec(memory_space=pltpu.VMEM)
    out, count = pl.pallas_call(
        functools.partial(kernel, blks, grps, (channels, segs, bins, half), splits == 1),
        out_shape=(
            pltpu.VMEM((LAGS, STEPS, channels, block), jnp.bfloat16),
            jax.ShapeDtypeStruct((channels, STEPS * block), jnp.float32),
        ),
        in_specs=[vmem] * 3 + [pl.BlockSpec(memory_space=pltpu.HBM)] * 2,
        out_specs=(vmem, vmem),
        scratch_shapes=[
            pltpu.VMEM((length, 2 * bins), jnp.bfloat16),
            pltpu.VMEM((segs * LANES, segs * LANES), jnp.bfloat16),
            pltpu.VMEM((LAGS, 2 * half), jnp.bfloat16),
            pltpu.SemaphoreType.DMA((2,)),
            pltpu.VMEM((STEPS, grps, channels, width), jnp.bfloat16),
            pltpu.VMEM((half // GROUP, channels * GROUP, 2 * segs * GROUP), jnp.bfloat16),
            pltpu.VMEM((channels // 2, 2, half, 2 * block), jnp.bfloat16),
            pltpu.VMEM((channels // 2, 2 * block), jnp.float32),
            pltpu.VMEM((channels, LANES), jnp.float32),
            pltpu.VMEM(((LAGS + 1) * channels, block), jnp.float32),
            pltpu.SemaphoreType.DMA((STEPS, PIECES, grps)),
            pltpu.SemaphoreType.DMA((STEPS - 1, PIECES, 2)),
            pltpu.SemaphoreType.DMA((STEPS, PIECES, 3)),
            pltpu.SemaphoreType.DMA((STEPS, PIECES, grps // 2)),
        ],
        compiler_params=pltpu.CompilerParams(
            collective_id=0, has_side_effects=True, vmem_limit_bytes=52 * 1024 * 1024
        ),
    )(
        records.reshape(channels * segs, length),
        flags.T,
        jnp.asarray(row_table(channels, segs)),
        high.reshape(length, 2 * bins),
        lags.reshape(LAGS, 2 * half),
    )
    out = out.transpose(0, 2, 1, 3)
    if splits > 1:
        out = lax.psum_scatter(out, "sub", scatter_dimension=0, tiled=True).astype(jnp.float32)
        out = (out / jnp.sqrt(bins * jnp.maximum(count, 1.0)).reshape(1, channels, STEPS, block)).astype(jnp.bfloat16)
    return out


def solution(mesh):
    return jax.shard_map(
        on_device,
        mesh=mesh,
        in_specs=(P(("dom", "blk", "grp"), None, None), P(("dom", "blk", "grp"), None)),
        out_specs=P("sub", ("dom", "blk", "grp"), None, None),
        check_vma=False,
    )
```

```python
import functools

import jax
import jax.numpy as jnp
import ml_dtypes
import numpy as np
from jax import lax
from jax.experimental import pallas as pl
from jax.experimental.pallas import tpu as pltpu
from jax.sharding import PartitionSpec as P

LAGS = 256
STEPS = 3
LANES = 128
GROUP = 16
SPLIT = (0, 1, 2)
PIECES = len(SPLIT) - 1
CLIMB = ((1, 0), (1, 1), (2, 1))
ORDER = (
    ("s", 0), ("s", 1), ("f", 0), ("t", 0), ("b", 0), ("s", 2), ("f", 1), ("s", 3), ("c", 0), ("m", 0), ("s", 4), ("t", 1), ("f", 2), ("c", 1), ("t", 2), ("s", 5), ("b", 1), ("c", 2), ("m", 1), ("t", 3), ("f", 3), ("e", 0), ("e", 1), ("p", 0), ("c", 3), ("f", 4), ("m", 2), ("t", 4), ("t", 5), ("f", 5), ("m", 3), ("c", 4), ("e", 2), ("e", 3), ("p", 1), ("c", 5), ("m", 4), ("g", 0), ("g", 1), ("m", 5), ("e", 4), ("p", 2),
)
MESH = pl.DeviceIdType.MESH


def dft_tables(length):
    bins = length // 2
    phase = np.mod(np.arange(length)[:, None] * np.arange(bins)[None, :], length)
    angle = 2.0 * np.pi * phase / length
    return np.cos(angle).astype(np.float32), (-np.sin(angle)).astype(np.float32)


def lag_tables(length):
    bins = length // 2
    phase = np.mod((np.arange(LAGS) - LAGS // 2)[:, None] * np.arange(bins)[None, :], length)
    angle = 2.0 * np.pi * phase / length
    both = np.stack([np.cos(angle), -np.sin(angle)], axis=1).astype(np.float32)
    return both.astype(ml_dtypes.bfloat16)


def row_table(channels, segs):
    table = np.zeros((segs, channels, channels, segs), np.float32)
    for s in range(segs):
        for c in range(channels):
            table[s, c, c, s] = 1.0
    size = segs * channels
    return table.reshape(size, size).astype(ml_dtypes.bfloat16)


def mm(a, b):
    return jnp.dot(a, b, preferred_element_type=jnp.float32)


def mm_t(a, b):
    return lax.dot_general(a, b, (((1,), (1,)), ((), ())), preferred_element_type=jnp.float32)


def kernel(
    blks, grps, dims, normalise,
    rec_ref, flag_ref, row_ref, hi_hbm, lag_hbm,
    out_ref, count_ref,
    hi_ref, perm_ref, lag_ref, load_sem, buf, diag, cross, inv, wide, stage, acc, recv_sem, hop_sem, peer_sem, sib_sem,
):
    channels, segs, bins, half = dims
    width = half * 2 * segs
    chunks = half // GROUP
    pair = channels // 2
    loads = [
        pltpu.make_async_copy(source, target, load_sem.at[n])
        for n, (source, target) in enumerate(
            ((hi_hbm, hi_ref), (lag_hbm, lag_ref)))
    ]
    for load in loads[:-1]:
        load.start()
    b = lax.axis_index("blk")
    g = lax.axis_index("grp")
    sib = g + 1 - 2 * lax.rem(g, 2)
    core = lax.rem(g, 2)
    across = g + 2 - 4 * lax.rem(g // 2, 2)
    along = g + 4 - 8 * lax.rem(g // 4, 2)
    source = (1 - core) * across + core * along
    target = core * across + (1 - core) * along
    corner = across + along - g
    held = (g, source, target, corner)

    barrier = pltpu.get_barrier_semaphore()
    pl.semaphore_signal(barrier, inc=1, device_id={"blk": lax.rem(b + blks - 1, blks)}, device_id_type=MESH)
    for other in (across, along, sib):
        pl.semaphore_signal(barrier, inc=1, device_id={"grp": other}, device_id_type=MESH)

    per = LANES // GROUP
    came = lax.broadcasted_iota(jnp.int32, (segs * LANES, 1), 0)
    goes = came // GROUP % per * LANES + came // LANES * GROUP + came % GROUP
    lane = lax.broadcasted_iota(jnp.int32, (segs * LANES, LANES), 1)
    for q in range(per):
        perm_ref[:, q * LANES:(q + 1) * LANES] = jnp.where(goes == lane + q * LANES, 1.0, 0.0).astype(jnp.bfloat16)
    rec = mm(row_ref[...], rec_ref[...]).astype(jnp.bfloat16)
    loads[0].wait()
    spec = mm(rec, hi_ref[...])
    real = spec[:, :bins]
    imag = spec[:, bins:]
    power = real * real + imag * imag
    level = jnp.sum(power, axis=1, keepdims=True) / bins
    scale = 1.0 / jnp.sqrt(power[:, :half] + level + 1e-06)
    wide[...] = jnp.zeros_like(wide)
    unit = (lax.broadcasted_iota(jnp.int32, (channels, channels), 0)
            == lax.broadcasted_iota(jnp.int32, (channels, channels), 1)).astype(jnp.float32)
    wide[:, :segs] = mm_t(unit, flag_ref[...].astype(jnp.float32))
    flags = wide[...]
    pieces = [(real[:, :half] * scale).astype(jnp.bfloat16), (imag[:, :half] * scale).astype(jnp.bfloat16)]
    rows = []
    for t in range(half // LANES):
        for piece in pieces:
            rows.append(jnp.concatenate([
                piece[s * channels:(s + 1) * channels, t * LANES:(t + 1) * LANES]
                * flags[:, s:s + 1].astype(jnp.bfloat16)
                for s in range(segs)
            ], axis=1))
    regrouped = mm(jnp.concatenate(rows, axis=0), perm_ref[...]).astype(jnp.bfloat16)
    for t in range(half // LANES):
        for i in range(2):
            part = regrouped[(t * 2 + i) * channels:(t * 2 + i + 1) * channels]
            for q in range(per):
                at = ((t * per + q) * 2 + i) * LANES
                buf[0, g, :, at:at + LANES] = part[:, q * LANES:(q + 1) * LANES]
    buf[0, g, :, width:width + LANES] = flags.astype(jnp.bfloat16)

    loads[-1].start()
    pl.semaphore_wait(barrier, 4)

    sent = []

    bounds = [chunks * part // SPLIT[-1] for part in SPLIT]
    edges = [2 * segs * GROUP * bound for bound in bounds[:-1]] + [width + LANES]
    spans = [(low, high - low) for low, high in zip(edges[:-1], edges[1:])]
    steps = [(k, h) for k in range(STEPS) for h in range(PIECES)]

    def piece(k, h, slot):
        return buf.at[k, slot, :, pl.ds(*spans[h])]

    def send(source, target, send_sem, landed, where):
        copy = pltpu.make_async_remote_copy(
            src_ref=source, dst_ref=target, send_sem=send_sem, recv_sem=landed,
            device_id=where, device_id_type=MESH,
        )
        copy.start()
        sent.append(copy)

    def arrived(k, h, slot):
        ref = piece(k, h, slot)
        pltpu.make_async_copy(ref, ref, recv_sem.at[k, h, slot]).wait()

    def give(k, h, slot, n, other, sem):
        ref = piece(k, h, slot)
        send(ref, ref, sem.at[k, h, n], recv_sem.at[k, h, slot], {"grp": other})

    def rise(k, h, slot, n):
        send(piece(k, h, slot), piece(k + 1, h, slot), hop_sem.at[k, h, n], recv_sem.at[k + 1, h, slot],
             {"blk": lax.rem(b + 1, blks)})

    def spread(n):
        k, h = steps[n]
        if k:
            arrived(k, h, g)
        if k + 1 < STEPS:
            rise(k, h, g, 0)
        give(k, h, g, 0, target, peer_sem)
        give(k, h, g, 1, source, peer_sem)
        give(k, h, g, 0, sib, sib_sem)

    def forward(n):
        k, h = steps[n]
        arrived(k, h, source)
        if (k, h) not in CLIMB:
            give(k, h, source, 2, target, peer_sem)
        give(k, h, source, 1, sib, sib_sem)

    def relay(n):
        k, h = steps[n]
        arrived(k, h, target)
        give(k, h, target, 2, sib, sib_sem)

    def finish(n):
        k, h = steps[n]
        arrived(k, h, corner)
        if (k + 1, h) in CLIMB:
            rise(k, h, corner, 1)
        give(k, h, corner, 3, sib, sib_sem)

    def gather(n):
        k, h = steps[n]
        for slot in held:
            arrived(k, h, slot + 1 - 2 * lax.rem(slot, 2))

    size = 2 * segs * GROUP
    few = GROUP // 2
    same = (lax.broadcasted_iota(jnp.int32, (channels * few, size), 0) % few
            == lax.broadcasted_iota(jnp.int32, (channels * few, size), 1) % few)

    def build(q, carry):
        at = pl.multiple_of(q * size, size)
        first = buf[0, g, :, pl.ds(at, size)].astype(jnp.float32)
        second = jnp.concatenate([first[:, LANES:], -first[:, :LANES]], axis=1)
        for i, value in enumerate((first, second)):
            wide = jnp.broadcast_to(value[:, None, :], (channels, few, size)).reshape(channels * few, size)
            diag[q, i * channels * few:(i + 1) * channels * few, :] = jnp.where(same, wide, 0.0).astype(jnp.bfloat16)
        return carry

    block = grps * channels
    upper = lax.broadcasted_iota(jnp.int32, (block, size), 1) % GROUP >= few

    def multiply(q, k):
        other = buf[k, :, :, q * size:(q + 1) * size].reshape(block, size)
        zero = jnp.zeros_like(other)
        other = jnp.concatenate([jnp.where(upper, zero, other), jnp.where(upper, other, zero)], axis=0)
        product = mm_t(diag[q], other).reshape(2, 2, pair, few, 2 * block)
        product = jnp.concatenate([product[..., :block], product[..., block:]], axis=3).astype(jnp.bfloat16)
        for i in range(2):
            for p in range(2):
                cross[:, i, q * GROUP:(q + 1) * GROUP, p * block:(p + 1) * block] = product[i, p]

    begun = bounds[-2] * GROUP // LANES * LANES

    def table(low, high):
        return jnp.concatenate([lag_ref[:, i * half + low:i * half + high] for i in range(2)], axis=1)

    def early(j):
        if begun:
            for c in range(j * pair // 2, (j + 1) * pair // 2):
                acc[c] = mm(table(0, begun), cross[c, :, :begun].reshape(2 * begun, 2 * block))

    def lag(c, k):
        if begun and k == STEPS - 1:
            total = acc[c] + mm(table(begun, half), cross[c, :, begun:].reshape(2 * (half - begun), 2 * block))
        else:
            total = mm(lag_ref[...], cross[c].reshape(2 * half, 2 * block))
        if normalise:
            total = total * inv[c:c + 1, :]
        stage[pl.ds(c, LAGS, stride=channels), :] = total[:, :block]
        stage[pl.ds(c + pair, LAGS, stride=channels), :] = total[:, block:]

    def place(k):
        for n in range(LAGS // 16):
            part = stage[n * 16 * channels:(n + 1) * 16 * channels, :]
            out_ref[n * 16:(n + 1) * 16, k] = part.astype(jnp.bfloat16).reshape(16, channels, block)

    def prepare(n):
        lax.fori_loop(bounds[n], bounds[n + 1], build, 0, unroll=2)

    def combine(n):
        k, h = steps[n]
        gather(n)
        for q in range(bounds[h], bounds[h + 1]):
            multiply(q, k)

    def emit(n):
        k = n // 2
        if n == 0:
            loads[-1].wait()
        if n % 2 == 0:
            tile = buf[k, :, :, width:width + LANES].reshape(block, LANES)
            count = mm_t(flags.astype(jnp.bfloat16), tile)
            count_ref[:, k * block:(k + 1) * block] = count
            factor = lax.rsqrt(bins * jnp.maximum(count, 1.0))
            inv[:, :block] = factor[:pair]
            inv[:, block:] = factor[pair:]
        if k < STEPS - 1:
            span = range(n % 2 * pair // 2, (n % 2 + 1) * pair // 2)
        else:
            span = range(pair)
        for c in span:
            lag(c, k)

    acts = {"s": spread, "f": forward, "t": relay, "c": finish, "b": prepare, "m": combine, "e": emit, "g": early, "p": place}
    for act, n in ORDER:
        acts[act](n)

    for copy in sent:
        copy.wait_send()


def on_device(records, flags):
    channels, segs, length = records.shape
    bins = length // 2
    splits = lax.axis_size("sub")
    blks = lax.axis_size("blk")
    grps = lax.axis_size("grp")
    half = bins // splits
    block = grps * channels
    cos, sin = dft_tables(length)
    lags = lag_tables(length)
    both = np.stack([cos, sin], axis=1)
    high = both.astype(ml_dtypes.bfloat16)
    high, lags = jnp.asarray(high), jnp.asarray(lags)
    if splits > 1:
        first = lax.axis_index("sub") * half
        high = jnp.roll(high, -first, axis=2)
        lags = lax.dynamic_slice_in_dim(lags, first, half, 2)
    width = half * 2 * segs + LANES
    vmem = pl.BlockSpec(memory_space=pltpu.VMEM)
    out, count = pl.pallas_call(
        functools.partial(kernel, blks, grps, (channels, segs, bins, half), splits == 1),
        out_shape=(
            pltpu.VMEM((LAGS, STEPS, channels, block), jnp.bfloat16),
            jax.ShapeDtypeStruct((channels, STEPS * block), jnp.float32),
        ),
        in_specs=[vmem] * 3 + [pl.BlockSpec(memory_space=pltpu.HBM)] * 2,
        out_specs=(vmem, vmem),
        scratch_shapes=[
            pltpu.VMEM((length, 2 * bins), jnp.bfloat16),
            pltpu.VMEM((segs * LANES, segs * LANES), jnp.bfloat16),
            pltpu.VMEM((LAGS, 2 * half), jnp.bfloat16),
            pltpu.SemaphoreType.DMA((2,)),
            pltpu.VMEM((STEPS, grps, channels, width), jnp.bfloat16),
            pltpu.VMEM((half // GROUP, channels * GROUP, 2 * segs * GROUP), jnp.bfloat16),
            pltpu.VMEM((channels // 2, 2, half, 2 * block), jnp.bfloat16),
            pltpu.VMEM((channels // 2, 2 * block), jnp.float32),
            pltpu.VMEM((channels, LANES), jnp.float32),
            pltpu.VMEM(((LAGS + 1) * channels, block), jnp.float32),
            pltpu.VMEM((channels // 2, LAGS, 2 * block), jnp.float32),
            pltpu.SemaphoreType.DMA((STEPS, PIECES, grps)),
            pltpu.SemaphoreType.DMA((STEPS - 1, PIECES, 2)),
            pltpu.SemaphoreType.DMA((STEPS, PIECES, 3)),
            pltpu.SemaphoreType.DMA((STEPS, PIECES, grps // 2)),
        ],
        compiler_params=pltpu.CompilerParams(
            collective_id=0, has_side_effects=True, vmem_limit_bytes=52 * 1024 * 1024
        ),
    )(
        records.reshape(channels * segs, length),
        flags.T,
        jnp.asarray(row_table(channels, segs)),
        high.reshape(length, 2 * bins),
        lags.reshape(LAGS, 2 * half),
    )
    out = out.transpose(0, 2, 1, 3)
    if splits > 1:
        out = lax.psum_scatter(out, "sub", scatter_dimension=0, tiled=True).astype(jnp.float32)
        out = (out / jnp.sqrt(bins * jnp.maximum(count, 1.0)).reshape(1, channels, STEPS, block)).astype(jnp.bfloat16)
    return out


def solution(mesh):
    return jax.shard_map(
        on_device,
        mesh=mesh,
        in_specs=(P(("dom", "blk", "grp"), None, None), P(("dom", "blk", "grp"), None)),
        out_specs=P("sub", ("dom", "blk", "grp"), None, None),
        check_vma=False,
    )
```

```python
import functools

import jax
import jax.numpy as jnp
import ml_dtypes
import numpy as np
from jax import lax
from jax.experimental import pallas as pl
from jax.experimental.pallas import tpu as pltpu
from jax.sharding import PartitionSpec as P

LAGS = 256
STEPS = 3
LANES = 128
GROUP = 16
TURNS = 4
SPLIT = (0, 1, 2)
PIECES = len(SPLIT) - 1
CLIMB = ((1, 0), (1, 1), (2, 1))
ORDER = (
    ("s", 0), ("s", 1), ("f", 0), ("t", 0), ("b", 0), ("s", 2), ("f", 1), ("s", 3), ("c", 0), ("m", 0), ("s", 4), ("t", 1), ("f", 2), ("c", 1), ("t", 2), ("s", 5), ("b", 1), ("c", 2), ("m", 1), ("t", 3), ("f", 3), ("e", 0), ("e", 1), ("p", 0), ("c", 3), ("f", 4), ("m", 2), ("t", 4), ("t", 5), ("f", 5), ("m", 3), ("c", 4), ("e", 2), ("e", 3), ("p", 1), ("c", 5), ("m", 4), ("g", 0), ("g", 1), ("m", 5), ("e", 4), ("p", 2),
)
MESH = pl.DeviceIdType.MESH


def dft_tables(length):
    bins = length // 2
    phase = np.mod(np.arange(length)[:, None] * np.arange(bins)[None, :], length)
    angle = 2.0 * np.pi * phase / length
    return np.cos(angle).astype(np.float32), (-np.sin(angle)).astype(np.float32)


def lag_tables(length):
    bins = length // 2
    phase = np.mod((np.arange(LAGS) - LAGS // 2)[:, None] * np.arange(bins)[None, :], length)
    angle = 2.0 * np.pi * phase / length
    both = np.stack([np.cos(angle), -np.sin(angle)], axis=1).astype(np.float32)
    return both.astype(ml_dtypes.bfloat16)


def mm(a, b):
    return jnp.dot(a, b, preferred_element_type=jnp.float32)


def mm_t(a, b):
    return lax.dot_general(a, b, (((1,), (1,)), ((), ())), preferred_element_type=jnp.float32)


def kernel(
    blks, grps, dims, normalise,
    rec_hbm, flag_hbm, hi_hbm, lag_hbm,
    out_ref, count_ref,
    rec_ref, flag_ref, hi_ref, perm_ref, lag_ref, load_sem, buf, diag, cross, inv, wide, stage, acc, recv_sem, hop_sem, peer_sem, sib_sem,
):
    channels, segs, bins, half = dims
    width = half * 2 * segs
    chunks = half // GROUP
    pair = channels // 2
    depth = hi_hbm.shape[0] // TURNS
    parts = [pl.ds(n * depth, depth) for n in range(TURNS)]
    loads = [
        pltpu.make_async_copy(source, target, load_sem.at[n])
        for n, (source, target) in enumerate(
            [(rec_hbm, rec_ref), (flag_hbm, flag_ref)]
            + [(hi_hbm.at[rows], hi_ref.at[rows]) for rows in parts] + [(lag_hbm, lag_ref)])
    ]
    for load in loads[:-1]:
        load.start()
    b = lax.axis_index("blk")
    g = lax.axis_index("grp")
    sib = g + 1 - 2 * lax.rem(g, 2)
    core = lax.rem(g, 2)
    across = g + 2 - 4 * lax.rem(g // 2, 2)
    along = g + 4 - 8 * lax.rem(g // 4, 2)
    source = (1 - core) * across + core * along
    target = core * across + (1 - core) * along
    corner = across + along - g
    held = (g, source, target, corner)

    barrier = pltpu.get_barrier_semaphore()
    pl.semaphore_signal(barrier, inc=1, device_id={"blk": lax.rem(b + blks - 1, blks)}, device_id_type=MESH)
    for other in (across, along, sib):
        pl.semaphore_signal(barrier, inc=1, device_id={"grp": other}, device_id_type=MESH)

    per = LANES // GROUP
    came = lax.broadcasted_iota(jnp.int32, (segs * LANES, 1), 0)
    goes = came // GROUP % per * LANES + came // LANES * GROUP + came % GROUP
    lane = lax.broadcasted_iota(jnp.int32, (segs * LANES, LANES), 1)
    for q in range(per):
        perm_ref[:, q * LANES:(q + 1) * LANES] = jnp.where(goes == lane + q * LANES, 1.0, 0.0).astype(jnp.bfloat16)
    came = lax.broadcasted_iota(jnp.int32, (segs * channels, segs * channels), 0)
    goes = came % channels * segs + came // channels
    order = jnp.where(goes == lax.broadcasted_iota(jnp.int32, came.shape, 1), 1.0, 0.0).astype(jnp.bfloat16)
    loads[0].wait()
    rec = mm(order, rec_ref[...]).astype(jnp.bfloat16)
    spec = 0.0
    for n in range(TURNS):
        loads[2 + n].wait()
        spec = spec + mm(rec[:, n * depth:(n + 1) * depth], hi_ref[parts[n]])
    loads[1].wait()
    real = spec[:, :bins]
    imag = spec[:, bins:]
    power = real * real + imag * imag
    level = jnp.sum(power, axis=1, keepdims=True) / bins
    scale = 1.0 / jnp.sqrt(power[:, :half] + level + 1e-06)
    wide[...] = jnp.zeros_like(wide)
    unit = (lax.broadcasted_iota(jnp.int32, (channels, channels), 0)
            == lax.broadcasted_iota(jnp.int32, (channels, channels), 1)).astype(jnp.float32)
    wide[:, :segs] = mm_t(unit, flag_ref[...].astype(jnp.float32))
    flags = wide[...]
    pieces = [(real[:, :half] * scale).astype(jnp.bfloat16), (imag[:, :half] * scale).astype(jnp.bfloat16)]
    rows = []
    for t in range(half // LANES):
        for piece in pieces:
            rows.append(jnp.concatenate([
                piece[s * channels:(s + 1) * channels, t * LANES:(t + 1) * LANES]
                * flags[:, s:s + 1].astype(jnp.bfloat16)
                for s in range(segs)
            ], axis=1))
    regrouped = mm(jnp.concatenate(rows, axis=0), perm_ref[...]).astype(jnp.bfloat16)
    for t in range(half // LANES):
        for i in range(2):
            part = regrouped[(t * 2 + i) * channels:(t * 2 + i + 1) * channels]
            for q in range(per):
                at = ((t * per + q) * 2 + i) * LANES
                buf[0, g, :, at:at + LANES] = part[:, q * LANES:(q + 1) * LANES]
    buf[0, g, :, width:width + LANES] = flags.astype(jnp.bfloat16)

    loads[-1].start()
    pl.semaphore_wait(barrier, 4)

    sent = []

    bounds = [chunks * part // SPLIT[-1] for part in SPLIT]
    edges = [2 * segs * GROUP * bound for bound in bounds[:-1]] + [width + LANES]
    spans = [(low, high - low) for low, high in zip(edges[:-1], edges[1:])]
    steps = [(k, h) for k in range(STEPS) for h in range(PIECES)]

    def piece(k, h, slot):
        return buf.at[k, slot, :, pl.ds(*spans[h])]

    def send(source, target, send_sem, landed, where):
        copy = pltpu.make_async_remote_copy(
            src_ref=source, dst_ref=target, send_sem=send_sem, recv_sem=landed,
            device_id=where, device_id_type=MESH,
        )
        copy.start()
        sent.append(copy)

    def arrived(k, h, slot):
        ref = piece(k, h, slot)
        pltpu.make_async_copy(ref, ref, recv_sem.at[k, h, slot]).wait()

    def give(k, h, slot, n, other, sem):
        ref = piece(k, h, slot)
        send(ref, ref, sem.at[k, h, n], recv_sem.at[k, h, slot], {"grp": other})

    def rise(k, h, slot, n):
        send(piece(k, h, slot), piece(k + 1, h, slot), hop_sem.at[k, h, n], recv_sem.at[k + 1, h, slot],
             {"blk": lax.rem(b + 1, blks)})

    def spread(n):
        k, h = steps[n]
        if k:
            arrived(k, h, g)
        if k + 1 < STEPS:
            rise(k, h, g, 0)
        give(k, h, g, 0, target, peer_sem)
        give(k, h, g, 1, source, peer_sem)
        give(k, h, g, 0, sib, sib_sem)

    def forward(n):
        k, h = steps[n]
        arrived(k, h, source)
        if (k, h) not in CLIMB:
            give(k, h, source, 2, target, peer_sem)
        give(k, h, source, 1, sib, sib_sem)

    def relay(n):
        k, h = steps[n]
        arrived(k, h, target)
        give(k, h, target, 2, sib, sib_sem)

    def finish(n):
        k, h = steps[n]
        arrived(k, h, corner)
        if (k + 1, h) in CLIMB:
            rise(k, h, corner, 1)
        give(k, h, corner, 3, sib, sib_sem)

    def gather(n):
        k, h = steps[n]
        for slot in held:
            arrived(k, h, slot + 1 - 2 * lax.rem(slot, 2))

    size = 2 * segs * GROUP
    few = GROUP // 2
    same = (lax.broadcasted_iota(jnp.int32, (channels * few, size), 0) % few
            == lax.broadcasted_iota(jnp.int32, (channels * few, size), 1) % few)

    def build(q, carry):
        at = pl.multiple_of(q * size, size)
        first = buf[0, g, :, pl.ds(at, size)].astype(jnp.float32)
        second = jnp.concatenate([first[:, LANES:], -first[:, :LANES]], axis=1)
        for i, value in enumerate((first, second)):
            wide = jnp.broadcast_to(value[:, None, :], (channels, few, size)).reshape(channels * few, size)
            diag[q, i * channels * few:(i + 1) * channels * few, :] = jnp.where(same, wide, 0.0).astype(jnp.bfloat16)
        return carry

    block = grps * channels
    upper = lax.broadcasted_iota(jnp.int32, (block, size), 1) % GROUP >= few

    def multiply(q, k):
        other = buf[k, :, :, q * size:(q + 1) * size].reshape(block, size)
        zero = jnp.zeros_like(other)
        other = jnp.concatenate([jnp.where(upper, zero, other), jnp.where(upper, other, zero)], axis=0)
        product = mm_t(diag[q], other).reshape(2, 2, pair, few, 2 * block)
        product = jnp.concatenate([product[..., :block], product[..., block:]], axis=3).astype(jnp.bfloat16)
        for i in range(2):
            for p in range(2):
                cross[:, i, q * GROUP:(q + 1) * GROUP, p * block:(p + 1) * block] = product[i, p]

    begun = bounds[-2] * GROUP // LANES * LANES

    def table(low, high):
        return jnp.concatenate([lag_ref[:, i * half + low:i * half + high] for i in range(2)], axis=1)

    def early(j):
        if begun:
            for c in range(j * pair // 2, (j + 1) * pair // 2):
                acc[c] = mm(table(0, begun), cross[c, :, :begun].reshape(2 * begun, 2 * block))

    def lag(c, k):
        if begun and k == STEPS - 1:
            total = acc[c] + mm(table(begun, half), cross[c, :, begun:].reshape(2 * (half - begun), 2 * block))
        else:
            total = mm(lag_ref[...], cross[c].reshape(2 * half, 2 * block))
        if normalise:
            total = total * inv[c:c + 1, :]
        stage[pl.ds(c, LAGS, stride=channels), :] = total[:, :block]
        stage[pl.ds(c + pair, LAGS, stride=channels), :] = total[:, block:]

    def place(k):
        for n in range(LAGS // 16):
            part = stage[n * 16 * channels:(n + 1) * 16 * channels, :]
            out_ref[n * 16:(n + 1) * 16, k] = part.astype(jnp.bfloat16).reshape(16, channels, block)

    def prepare(n):
        lax.fori_loop(bounds[n], bounds[n + 1], build, 0, unroll=2)

    def combine(n):
        k, h = steps[n]
        gather(n)
        for q in range(bounds[h], bounds[h + 1]):
            multiply(q, k)

    def emit(n):
        k = n // 2
        if n == 0:
            loads[-1].wait()
        if n % 2 == 0:
            tile = buf[k, :, :, width:width + LANES].reshape(block, LANES)
            count = mm_t(flags.astype(jnp.bfloat16), tile)
            count_ref[:, k * block:(k + 1) * block] = count
            factor = lax.rsqrt(bins * jnp.maximum(count, 1.0))
            inv[:, :block] = factor[:pair]
            inv[:, block:] = factor[pair:]
        if k < STEPS - 1:
            span = range(n % 2 * pair // 2, (n % 2 + 1) * pair // 2)
        else:
            span = range(pair)
        for c in span:
            lag(c, k)

    acts = {"s": spread, "f": forward, "t": relay, "c": finish, "b": prepare, "m": combine, "e": emit, "g": early, "p": place}
    for act, n in ORDER:
        acts[act](n)

    for copy in sent:
        copy.wait_send()


def on_device(records, flags):
    channels, segs, length = records.shape
    bins = length // 2
    splits = lax.axis_size("sub")
    blks = lax.axis_size("blk")
    grps = lax.axis_size("grp")
    half = bins // splits
    block = grps * channels
    cos, sin = dft_tables(length)
    lags = lag_tables(length)
    both = np.stack([cos, sin], axis=1)
    high = both.astype(ml_dtypes.bfloat16)
    high, lags = jnp.asarray(high), jnp.asarray(lags)
    if splits > 1:
        first = lax.axis_index("sub") * half
        high = jnp.roll(high, -first, axis=2)
        lags = lax.dynamic_slice_in_dim(lags, first, half, 2)
    width = half * 2 * segs + LANES
    vmem = pl.BlockSpec(memory_space=pltpu.VMEM)
    out, count = pl.pallas_call(
        functools.partial(kernel, blks, grps, (channels, segs, bins, half), splits == 1),
        out_shape=(
            pltpu.VMEM((LAGS, STEPS, channels, block), jnp.bfloat16),
            pltpu.VMEM((channels, STEPS * block), jnp.float32),
        ),
        in_specs=[pl.BlockSpec(memory_space=pltpu.HBM)] * 4,
        out_specs=(vmem, vmem),
        scratch_shapes=[
            pltpu.VMEM((channels * segs, length), jnp.bfloat16),
            pltpu.VMEM((segs, channels), jnp.int32),
            pltpu.VMEM((length, 2 * bins), jnp.bfloat16),
            pltpu.VMEM((segs * LANES, segs * LANES), jnp.bfloat16),
            pltpu.VMEM((LAGS, 2 * half), jnp.bfloat16),
            pltpu.SemaphoreType.DMA((3 + TURNS,)),
            pltpu.VMEM((STEPS, grps, channels, width), jnp.bfloat16),
            pltpu.VMEM((half // GROUP, channels * GROUP, 2 * segs * GROUP), jnp.bfloat16),
            pltpu.VMEM((channels // 2, 2, half, 2 * block), jnp.bfloat16),
            pltpu.VMEM((channels // 2, 2 * block), jnp.float32),
            pltpu.VMEM((channels, LANES), jnp.float32),
            pltpu.VMEM(((LAGS + 1) * channels, block), jnp.float32),
            pltpu.VMEM((channels // 2, LAGS, 2 * block), jnp.float32),
            pltpu.SemaphoreType.DMA((STEPS, PIECES, grps)),
            pltpu.SemaphoreType.DMA((STEPS - 1, PIECES, 2)),
            pltpu.SemaphoreType.DMA((STEPS, PIECES, 3)),
            pltpu.SemaphoreType.DMA((STEPS, PIECES, grps // 2)),
        ],
        compiler_params=pltpu.CompilerParams(
            collective_id=0, has_side_effects=True, vmem_limit_bytes=52 * 1024 * 1024
        ),
    )(
        records.reshape(channels * segs, length),
        flags.T,
        high.reshape(length, 2 * bins),
        lags.reshape(LAGS, 2 * half),
    )
    out = out.transpose(0, 2, 1, 3)
    if splits > 1:
        out = lax.psum_scatter(out, "sub", scatter_dimension=0, tiled=True).astype(jnp.float32)
        out = (out / jnp.sqrt(bins * jnp.maximum(count, 1.0)).reshape(1, channels, STEPS, block)).astype(jnp.bfloat16)
    return out


def solution(mesh):
    return jax.shard_map(
        on_device,
        mesh=mesh,
        in_specs=(P(("dom", "blk", "grp"), None, None), P(("dom", "blk", "grp"), None)),
        out_specs=P("sub", ("dom", "blk", "grp"), None, None),
        check_vma=False,
    )
```

```python
import functools

import jax
import jax.numpy as jnp
import ml_dtypes
import numpy as np
from jax import lax
from jax.experimental import pallas as pl
from jax.experimental.pallas import tpu as pltpu
from jax.sharding import PartitionSpec as P

LAGS = 256
STEPS = 3
LANES = 128
GROUP = 16
TURNS = 4
SPLIT = (0, 1, 2)
LAST = 4
PIECES = len(SPLIT) - 1
CLIMB = ((1, 0), (1, 1), (2, 1))
ORDER = (
    ("s", 0), ("s", 1), ("f", 0), ("t", 0), ("b", 0), ("s", 2), ("f", 1), ("s", 3), ("c", 0), ("m", 0), ("s", 4), ("t", 1), ("f", 2), ("c", 1), ("t", 2), ("s", 5), ("b", 1), ("c", 2), ("m", 1), ("t", 3), ("f", 3), ("e", 0), ("e", 1), ("p", 0), ("c", 3), ("f", 4), ("m", 2), ("t", 4), ("t", 5), ("f", 5), ("m", 3), ("c", 4), ("e", 2), ("e", 3), ("p", 1), ("c", 5), ("m", 4), ("g", 0), ("g", 1), ("m", 5), ("e", 4),
)
MESH = pl.DeviceIdType.MESH


def dft_tables(length):
    bins = length // 2
    phase = np.mod(np.arange(length)[:, None] * np.arange(bins)[None, :], length)
    angle = 2.0 * np.pi * phase / length
    return np.cos(angle).astype(np.float32), (-np.sin(angle)).astype(np.float32)


def lag_tables(length):
    bins = length // 2
    phase = np.mod((np.arange(LAGS) - LAGS // 2)[:, None] * np.arange(bins)[None, :], length)
    angle = 2.0 * np.pi * phase / length
    both = np.stack([np.cos(angle), -np.sin(angle)], axis=1).astype(np.float32)
    return both.astype(ml_dtypes.bfloat16)


def early_bins(half):
    return half // GROUP * SPLIT[-2] // SPLIT[-1] * GROUP // LANES * LANES


def columns(ref, half, low, high):
    return jnp.concatenate([ref[:, i * half + low:i * half + high] for i in range(2)], axis=1)


def mm(a, b):
    return jnp.dot(a, b, preferred_element_type=jnp.float32)


def mm_t(a, b):
    return lax.dot_general(a, b, (((1,), (1,)), ((), ())), preferred_element_type=jnp.float32)


def kernel(
    blks, grps, dims, normalise,
    rec_hbm, flag_hbm, hi_hbm, lag_hbm,
    out_ref, cross, acc, inv, lag_ref, count_ref,
    rec_ref, flag_ref, hi_ref, perm_ref, load_sem, buf, diag, wide, stage, recv_sem, hop_sem, peer_sem, sib_sem,
):
    channels, segs, bins, half = dims
    width = half * 2 * segs
    chunks = half // GROUP
    pair = channels // 2
    depth = hi_hbm.shape[0] // TURNS
    parts = [pl.ds(n * depth, depth) for n in range(TURNS)]
    loads = [
        pltpu.make_async_copy(source, target, load_sem.at[n])
        for n, (source, target) in enumerate(
            [(rec_hbm, rec_ref), (flag_hbm, flag_ref)]
            + [(hi_hbm.at[rows], hi_ref.at[rows]) for rows in parts] + [(lag_hbm, lag_ref)])
    ]
    for load in loads[:-1]:
        load.start()
    b = lax.axis_index("blk")
    g = lax.axis_index("grp")
    sib = g + 1 - 2 * lax.rem(g, 2)
    core = lax.rem(g, 2)
    across = g + 2 - 4 * lax.rem(g // 2, 2)
    along = g + 4 - 8 * lax.rem(g // 4, 2)
    source = (1 - core) * across + core * along
    target = core * across + (1 - core) * along
    corner = across + along - g
    held = (g, source, target, corner)

    barrier = pltpu.get_barrier_semaphore()
    pl.semaphore_signal(barrier, inc=1, device_id={"blk": lax.rem(b + blks - 1, blks)}, device_id_type=MESH)
    for other in (across, along, sib):
        pl.semaphore_signal(barrier, inc=1, device_id={"grp": other}, device_id_type=MESH)

    per = LANES // GROUP
    came = lax.broadcasted_iota(jnp.int32, (segs * LANES, 1), 0)
    goes = came // GROUP % per * LANES + came // LANES * GROUP + came % GROUP
    lane = lax.broadcasted_iota(jnp.int32, (segs * LANES, LANES), 1)
    for q in range(per):
        perm_ref[:, q * LANES:(q + 1) * LANES] = jnp.where(goes == lane + q * LANES, 1.0, 0.0).astype(jnp.bfloat16)
    came = lax.broadcasted_iota(jnp.int32, (segs * channels, segs * channels), 0)
    goes = came % channels * segs + came // channels
    order = jnp.where(goes == lax.broadcasted_iota(jnp.int32, came.shape, 1), 1.0, 0.0).astype(jnp.bfloat16)
    loads[0].wait()
    rec = mm(order, rec_ref[...]).astype(jnp.bfloat16)
    spec = 0.0
    for n in range(TURNS):
        loads[2 + n].wait()
        spec = spec + mm(rec[:, n * depth:(n + 1) * depth], hi_ref[parts[n]])
    loads[1].wait()
    real = spec[:, :bins]
    imag = spec[:, bins:]
    power = real * real + imag * imag
    level = jnp.sum(power, axis=1, keepdims=True) / bins
    scale = 1.0 / jnp.sqrt(power[:, :half] + level + 1e-06)
    wide[...] = jnp.zeros_like(wide)
    unit = (lax.broadcasted_iota(jnp.int32, (channels, channels), 0)
            == lax.broadcasted_iota(jnp.int32, (channels, channels), 1)).astype(jnp.float32)
    wide[:, :segs] = mm_t(unit, flag_ref[...].astype(jnp.float32))
    flags = wide[...]
    pieces = [(real[:, :half] * scale).astype(jnp.bfloat16), (imag[:, :half] * scale).astype(jnp.bfloat16)]
    rows = []
    for t in range(half // LANES):
        for piece in pieces:
            rows.append(jnp.concatenate([
                piece[s * channels:(s + 1) * channels, t * LANES:(t + 1) * LANES]
                * flags[:, s:s + 1].astype(jnp.bfloat16)
                for s in range(segs)
            ], axis=1))
    regrouped = mm(jnp.concatenate(rows, axis=0), perm_ref[...]).astype(jnp.bfloat16)
    for t in range(half // LANES):
        for i in range(2):
            part = regrouped[(t * 2 + i) * channels:(t * 2 + i + 1) * channels]
            for q in range(per):
                at = ((t * per + q) * 2 + i) * LANES
                buf[0, g, :, at:at + LANES] = part[:, q * LANES:(q + 1) * LANES]
    buf[0, g, :, width:width + LANES] = flags.astype(jnp.bfloat16)

    loads[-1].start()
    pl.semaphore_wait(barrier, 4)

    sent = []

    bounds = [chunks * part // SPLIT[-1] for part in SPLIT]
    edges = [2 * segs * GROUP * bound for bound in bounds[:-1]] + [width + LANES]
    spans = [(low, high - low) for low, high in zip(edges[:-1], edges[1:])]
    steps = [(k, h) for k in range(STEPS) for h in range(PIECES)]

    def piece(k, h, slot):
        return buf.at[k, slot, :, pl.ds(*spans[h])]

    def send(source, target, send_sem, landed, where):
        copy = pltpu.make_async_remote_copy(
            src_ref=source, dst_ref=target, send_sem=send_sem, recv_sem=landed,
            device_id=where, device_id_type=MESH,
        )
        copy.start()
        sent.append(copy)

    def arrived(k, h, slot):
        ref = piece(k, h, slot)
        pltpu.make_async_copy(ref, ref, recv_sem.at[k, h, slot]).wait()

    def give(k, h, slot, n, other, sem):
        ref = piece(k, h, slot)
        send(ref, ref, sem.at[k, h, n], recv_sem.at[k, h, slot], {"grp": other})

    def rise(k, h, slot, n):
        send(piece(k, h, slot), piece(k + 1, h, slot), hop_sem.at[k, h, n], recv_sem.at[k + 1, h, slot],
             {"blk": lax.rem(b + 1, blks)})

    def spread(n):
        k, h = steps[n]
        if k:
            arrived(k, h, g)
        if k + 1 < STEPS:
            rise(k, h, g, 0)
        give(k, h, g, 0, target, peer_sem)
        give(k, h, g, 1, source, peer_sem)
        give(k, h, g, 0, sib, sib_sem)

    def forward(n):
        k, h = steps[n]
        arrived(k, h, source)
        if (k, h) not in CLIMB:
            give(k, h, source, 2, target, peer_sem)
        give(k, h, source, 1, sib, sib_sem)

    def relay(n):
        k, h = steps[n]
        arrived(k, h, target)
        give(k, h, target, 2, sib, sib_sem)

    def finish(n):
        k, h = steps[n]
        arrived(k, h, corner)
        if (k + 1, h) in CLIMB:
            rise(k, h, corner, 1)
        give(k, h, corner, 3, sib, sib_sem)

    def gather(n):
        k, h = steps[n]
        for slot in held:
            arrived(k, h, slot + 1 - 2 * lax.rem(slot, 2))

    size = 2 * segs * GROUP
    few = GROUP // 2
    same = (lax.broadcasted_iota(jnp.int32, (channels * few, size), 0) % few
            == lax.broadcasted_iota(jnp.int32, (channels * few, size), 1) % few)

    def build(q, carry):
        at = pl.multiple_of(q * size, size)
        first = buf[0, g, :, pl.ds(at, size)].astype(jnp.float32)
        second = jnp.concatenate([first[:, LANES:], -first[:, :LANES]], axis=1)
        for i, value in enumerate((first, second)):
            wide = jnp.broadcast_to(value[:, None, :], (channels, few, size)).reshape(channels * few, size)
            diag[q, i * channels * few:(i + 1) * channels * few, :] = jnp.where(same, wide, 0.0).astype(jnp.bfloat16)
        return carry

    block = grps * channels
    upper = lax.broadcasted_iota(jnp.int32, (block, size), 1) % GROUP >= few

    def multiply(q, k):
        other = buf[k, :, :, q * size:(q + 1) * size].reshape(block, size)
        zero = jnp.zeros_like(other)
        other = jnp.concatenate([jnp.where(upper, zero, other), jnp.where(upper, other, zero)], axis=0)
        product = mm_t(diag[q], other).reshape(2, 2, pair, few, 2 * block)
        product = jnp.concatenate([product[..., :block], product[..., block:]], axis=3).astype(jnp.bfloat16)
        for i in range(2):
            for p in range(2):
                cross[:, i, q * GROUP:(q + 1) * GROUP, p * block:(p + 1) * block] = product[i, p]

    begun = early_bins(half)

    def early(j):
        if begun:
            for c in range(j * pair // 2, (j + 1) * pair // 2):
                acc[c] = mm(columns(lag_ref, half, 0, begun), cross[c, :, :begun].reshape(2 * begun, 2 * block))

    def lag(c):
        total = mm(lag_ref[...], cross[c].reshape(2 * half, 2 * block))
        if normalise:
            total = total * inv[c:c + 1, :]
        stage[pl.ds(c, LAGS, stride=channels), :] = total[:, :block]
        stage[pl.ds(c + pair, LAGS, stride=channels), :] = total[:, block:]

    def place(k):
        for n in range(LAGS // 16):
            part = stage[n * 16 * channels:(n + 1) * 16 * channels, :]
            out_ref[n * 16:(n + 1) * 16, k] = part.astype(jnp.bfloat16).reshape(16, channels, block)

    def prepare(n):
        lax.fori_loop(bounds[n], bounds[n + 1], build, 0, unroll=2)

    def combine(n):
        k, h = steps[n]
        gather(n)
        for q in range(bounds[h], bounds[h + 1]):
            multiply(q, k)

    def emit(n):
        k = n // 2
        if n == 0:
            loads[-1].wait()
        if n % 2 == 0:
            tile = buf[k, :, :, width:width + LANES].reshape(block, LANES)
            count = mm_t(flags.astype(jnp.bfloat16), tile)
            count_ref[:, k * block:(k + 1) * block] = count
            factor = lax.rsqrt(bins * jnp.maximum(count, 1.0))
            inv[:, :block] = factor[:pair]
            inv[:, block:] = factor[pair:]
        if k < STEPS - 1:
            for c in range(n % 2 * pair // 2, (n % 2 + 1) * pair // 2):
                lag(c)

    acts = {"s": spread, "f": forward, "t": relay, "c": finish, "b": prepare, "m": combine, "e": emit, "g": early, "p": place}
    for act, n in ORDER:
        acts[act](n)

    for copy in sent:
        copy.wait_send()


def last_kernel(normalise, first_ref, cross, acc, inv, lag_ref, out_hbm, stage, tail, sems):
    pair, half = cross.shape[0], cross.shape[2]
    channels, block = 2 * pair, cross.shape[3] // 2
    begun = early_bins(half)
    first = pltpu.make_async_copy(first_ref, out_hbm.at[:, pl.ds(0, STEPS - 1)], sems.at[LAST])
    first.start()
    for c in range(pair):
        total = mm(columns(lag_ref, half, begun, half), cross[c, :, begun:].reshape(2 * (half - begun), 2 * block))
        if begun:
            total = acc[c] + total
        if normalise:
            total = total * inv[c:c + 1, :]
        stage[pl.ds(c, LAGS, stride=channels), :] = total[:, :block]
        stage[pl.ds(c + pair, LAGS, stride=channels), :] = total[:, block:]
    span = LAGS // LAST
    copies = []
    for m in range(LAST):
        for n in range(m * span // 16, (m + 1) * span // 16):
            part = stage[n * 16 * channels:(n + 1) * 16 * channels, :]
            tail[n * 16:(n + 1) * 16] = part.astype(jnp.bfloat16).reshape(16, channels, block)
        rows = pl.ds(m * span, span)
        copies.append(pltpu.make_async_copy(tail.at[rows], out_hbm.at[rows, STEPS - 1], sems.at[m]))
        copies[-1].start()
    for copy in copies + [first]:
        copy.wait()


def on_device(records, flags):
    channels, segs, length = records.shape
    bins = length // 2
    splits = lax.axis_size("sub")
    blks = lax.axis_size("blk")
    grps = lax.axis_size("grp")
    half = bins // splits
    block = grps * channels
    cos, sin = dft_tables(length)
    lags = lag_tables(length)
    both = np.stack([cos, sin], axis=1)
    high = both.astype(ml_dtypes.bfloat16)
    high, lags = jnp.asarray(high), jnp.asarray(lags)
    if splits > 1:
        first = lax.axis_index("sub") * half
        high = jnp.roll(high, -first, axis=2)
        lags = lax.dynamic_slice_in_dim(lags, first, half, 2)
    width = half * 2 * segs + LANES
    vmem = pl.BlockSpec(memory_space=pltpu.VMEM)
    first, cross, acc, inv, lags, count = pl.pallas_call(
        functools.partial(kernel, blks, grps, (channels, segs, bins, half), splits == 1),
        out_shape=(
            pltpu.VMEM((LAGS, STEPS - 1, channels, block), jnp.bfloat16),
            pltpu.VMEM((channels // 2, 2, half, 2 * block), jnp.bfloat16),
            pltpu.VMEM((channels // 2, LAGS, 2 * block), jnp.float32),
            pltpu.VMEM((channels // 2, 2 * block), jnp.float32),
            pltpu.VMEM((LAGS, 2 * half), jnp.bfloat16),
            pltpu.VMEM((channels, STEPS * block), jnp.float32),
        ),
        in_specs=[pl.BlockSpec(memory_space=pltpu.HBM)] * 4,
        out_specs=(vmem,) * 6,
        scratch_shapes=[
            pltpu.VMEM((channels * segs, length), jnp.bfloat16),
            pltpu.VMEM((segs, channels), jnp.int32),
            pltpu.VMEM((length, 2 * bins), jnp.bfloat16),
            pltpu.VMEM((segs * LANES, segs * LANES), jnp.bfloat16),
            pltpu.SemaphoreType.DMA((3 + TURNS,)),
            pltpu.VMEM((STEPS, grps, channels, width), jnp.bfloat16),
            pltpu.VMEM((half // GROUP, channels * GROUP, 2 * segs * GROUP), jnp.bfloat16),
            pltpu.VMEM((channels, LANES), jnp.float32),
            pltpu.VMEM(((LAGS + 1) * channels, block), jnp.float32),
            pltpu.SemaphoreType.DMA((STEPS, PIECES, grps)),
            pltpu.SemaphoreType.DMA((STEPS - 1, PIECES, 2)),
            pltpu.SemaphoreType.DMA((STEPS, PIECES, 3)),
            pltpu.SemaphoreType.DMA((STEPS, PIECES, grps // 2)),
        ],
        compiler_params=pltpu.CompilerParams(
            collective_id=0, has_side_effects=True, vmem_limit_bytes=54 * 1024 * 1024
        ),
    )(
        records.reshape(channels * segs, length),
        flags.T,
        high.reshape(length, 2 * bins),
        lags.reshape(LAGS, 2 * half),
    )
    out = pl.pallas_call(
        functools.partial(last_kernel, splits == 1),
        out_shape=jax.ShapeDtypeStruct((LAGS, STEPS, channels, block), jnp.bfloat16),
        in_specs=[vmem] * 5,
        out_specs=pl.BlockSpec(memory_space=pltpu.HBM),
        scratch_shapes=[
            pltpu.VMEM(((LAGS + 1) * channels, block), jnp.float32),
            pltpu.VMEM((LAGS, channels, block), jnp.bfloat16),
            pltpu.SemaphoreType.DMA((LAST + 1,)),
        ],
        compiler_params=pltpu.CompilerParams(vmem_limit_bytes=32 * 1024 * 1024),
    )(first, cross, acc, inv, lags)
    out = out.transpose(0, 2, 1, 3)
    if splits > 1:
        out = lax.psum_scatter(out, "sub", scatter_dimension=0, tiled=True).astype(jnp.float32)
        out = (out / jnp.sqrt(bins * jnp.maximum(count, 1.0)).reshape(1, channels, STEPS, block)).astype(jnp.bfloat16)
    return out


def solution(mesh):
    return jax.shard_map(
        on_device,
        mesh=mesh,
        in_specs=(P(("dom", "blk", "grp"), None, None), P(("dom", "blk", "grp"), None)),
        out_specs=P("sub", ("dom", "blk", "grp"), None, None),
        check_vma=False,
    )
```

```python
import functools

import jax
import jax.numpy as jnp
import ml_dtypes
import numpy as np
from jax import lax
from jax.experimental import pallas as pl
from jax.experimental.pallas import tpu as pltpu
from jax.sharding import PartitionSpec as P

LAGS = 256
STEPS = 3
LANES = 128
GROUP = 16
TURNS = 4
SPLIT = (0, 1, 2)
LAST = 4
PIECES = len(SPLIT) - 1
CLIMB = ((1, 0), (1, 1), (2, 0))
ORDER = (
    ("s", 0), ("s", 1), ("f", 0), ("t", 0), ("b", 0), ("s", 2), ("f", 1), ("s", 3), ("c", 0), ("m", 0), ("s", 4), ("t", 1), ("f", 2), ("c", 1), ("t", 2), ("s", 5), ("b", 1), ("c", 2), ("m", 1), ("t", 3), ("f", 3), ("e", 0), ("e", 1), ("p", 0), ("c", 3), ("f", 4), ("m", 2), ("t", 4), ("t", 5), ("f", 5), ("m", 3), ("c", 4), ("e", 2), ("e", 3), ("p", 1), ("c", 5), ("m", 4), ("g", 0), ("g", 1), ("m", 5), ("e", 4),
)
MESH = pl.DeviceIdType.MESH


def dft_tables(length):
    bins = length // 2
    phase = np.mod(np.arange(length)[:, None] * np.arange(bins)[None, :], length)
    angle = 2.0 * np.pi * phase / length
    return np.cos(angle).astype(np.float32), (-np.sin(angle)).astype(np.float32)


def lag_tables(length):
    bins = length // 2
    phase = np.mod((np.arange(LAGS) - LAGS // 2)[:, None] * np.arange(bins)[None, :], length)
    angle = 2.0 * np.pi * phase / length
    both = np.stack([np.cos(angle), -np.sin(angle)], axis=1).astype(np.float32)
    return both.astype(ml_dtypes.bfloat16)


def early_bins(half):
    return half // GROUP * SPLIT[-2] // SPLIT[-1] * GROUP // LANES * LANES


def columns(ref, half, low, high):
    return jnp.concatenate([ref[:, i * half + low:i * half + high] for i in range(2)], axis=1)


def mm(a, b):
    return jnp.dot(a, b, preferred_element_type=jnp.float32)


def mm_t(a, b):
    return lax.dot_general(a, b, (((1,), (1,)), ((), ())), preferred_element_type=jnp.float32)


def kernel(
    blks, grps, dims, normalise,
    rec_hbm, flag_hbm, hi_hbm, lag_hbm,
    out_ref, cross, acc, inv, lag_ref, count_ref,
    rec_ref, flag_ref, hi_ref, perm_ref, load_sem, buf, diag, wide, stage, recv_sem, hop_sem, peer_sem, sib_sem,
):
    channels, segs, bins, half = dims
    width = half * 2 * segs
    chunks = half // GROUP
    pair = channels // 2
    depth = hi_hbm.shape[0] // TURNS
    parts = [pl.ds(n * depth, depth) for n in range(TURNS)]
    loads = [
        pltpu.make_async_copy(source, target, load_sem.at[n])
        for n, (source, target) in enumerate(
            [(rec_hbm, rec_ref), (flag_hbm, flag_ref)]
            + [(hi_hbm.at[rows], hi_ref.at[rows]) for rows in parts] + [(lag_hbm, lag_ref)])
    ]
    for load in loads[:-1]:
        load.start()
    b = lax.axis_index("blk")
    g = lax.axis_index("grp")
    sib = g + 1 - 2 * lax.rem(g, 2)
    core = lax.rem(g, 2)
    across = g + 2 - 4 * lax.rem(g // 2, 2)
    along = g + 4 - 8 * lax.rem(g // 4, 2)
    source = (1 - core) * across + core * along
    target = core * across + (1 - core) * along
    corner = across + along - g
    held = (g, source, target, corner)

    barrier = pltpu.get_barrier_semaphore()
    pl.semaphore_signal(barrier, inc=1, device_id={"blk": lax.rem(b + blks - 1, blks)}, device_id_type=MESH)
    for other in (across, along, sib):
        pl.semaphore_signal(barrier, inc=1, device_id={"grp": other}, device_id_type=MESH)

    per = LANES // GROUP
    came = lax.broadcasted_iota(jnp.int32, (segs * LANES, 1), 0)
    goes = came // GROUP % per * LANES + came // LANES * GROUP + came % GROUP
    lane = lax.broadcasted_iota(jnp.int32, (segs * LANES, LANES), 1)
    for q in range(per):
        perm_ref[:, q * LANES:(q + 1) * LANES] = jnp.where(goes == lane + q * LANES, 1.0, 0.0).astype(jnp.bfloat16)
    came = lax.broadcasted_iota(jnp.int32, (segs * channels, segs * channels), 0)
    goes = came % channels * segs + came // channels
    order = jnp.where(goes == lax.broadcasted_iota(jnp.int32, came.shape, 1), 1.0, 0.0).astype(jnp.bfloat16)
    loads[0].wait()
    rec = mm(order, rec_ref[...]).astype(jnp.bfloat16)
    spec = 0.0
    for n in range(TURNS):
        loads[2 + n].wait()
        spec = spec + mm(rec[:, n * depth:(n + 1) * depth], hi_ref[parts[n]])
    loads[1].wait()
    real = spec[:, :bins]
    imag = spec[:, bins:]
    power = real * real + imag * imag
    level = jnp.sum(power, axis=1, keepdims=True) / bins
    scale = 1.0 / jnp.sqrt(power[:, :half] + level + 1e-06)
    wide[...] = jnp.zeros_like(wide)
    unit = (lax.broadcasted_iota(jnp.int32, (channels, channels), 0)
            == lax.broadcasted_iota(jnp.int32, (channels, channels), 1)).astype(jnp.float32)
    wide[:, :segs] = mm_t(unit, flag_ref[...].astype(jnp.float32))
    flags = wide[...]
    pieces = [(real[:, :half] * scale).astype(jnp.bfloat16), (imag[:, :half] * scale).astype(jnp.bfloat16)]
    rows = []
    for t in range(half // LANES):
        for piece in pieces:
            rows.append(jnp.concatenate([
                piece[s * channels:(s + 1) * channels, t * LANES:(t + 1) * LANES]
                * flags[:, s:s + 1].astype(jnp.bfloat16)
                for s in range(segs)
            ], axis=1))
    regrouped = mm(jnp.concatenate(rows, axis=0), perm_ref[...]).astype(jnp.bfloat16)
    for t in range(half // LANES):
        for i in range(2):
            part = regrouped[(t * 2 + i) * channels:(t * 2 + i + 1) * channels]
            for q in range(per):
                at = ((t * per + q) * 2 + i) * LANES
                buf[0, g, :, at:at + LANES] = part[:, q * LANES:(q + 1) * LANES]
    buf[0, g, :, width:width + LANES] = flags.astype(jnp.bfloat16)

    loads[-1].start()
    pl.semaphore_wait(barrier, 4)

    sent = []

    bounds = [chunks * part // SPLIT[-1] for part in SPLIT]
    edges = [2 * segs * GROUP * bound for bound in bounds[:-1]] + [width + LANES]
    spans = [(low, high - low) for low, high in zip(edges[:-1], edges[1:])]
    steps = [(k, h) for k in range(STEPS) for h in range(PIECES)]

    def piece(k, h, slot):
        return buf.at[k, slot, :, pl.ds(*spans[h])]

    def send(source, target, send_sem, landed, where):
        copy = pltpu.make_async_remote_copy(
            src_ref=source, dst_ref=target, send_sem=send_sem, recv_sem=landed,
            device_id=where, device_id_type=MESH,
        )
        copy.start()
        sent.append(copy)

    def arrived(k, h, slot):
        ref = piece(k, h, slot)
        pltpu.make_async_copy(ref, ref, recv_sem.at[k, h, slot]).wait()

    def give(k, h, slot, n, other, sem):
        ref = piece(k, h, slot)
        send(ref, ref, sem.at[k, h, n], recv_sem.at[k, h, slot], {"grp": other})

    def rise(k, h, slot, n):
        send(piece(k, h, slot), piece(k + 1, h, slot), hop_sem.at[k, h, n], recv_sem.at[k + 1, h, slot],
             {"blk": lax.rem(b + 1, blks)})

    def spread(n):
        k, h = steps[n]
        if k:
            arrived(k, h, g)
        if k + 1 < STEPS:
            rise(k, h, g, 0)
        give(k, h, g, 0, target, peer_sem)
        give(k, h, g, 1, source, peer_sem)
        give(k, h, g, 0, sib, sib_sem)

    def forward(n):
        k, h = steps[n]
        arrived(k, h, source)
        if (k, h) not in CLIMB:
            give(k, h, source, 2, target, peer_sem)
        give(k, h, source, 1, sib, sib_sem)

    def relay(n):
        k, h = steps[n]
        arrived(k, h, target)
        give(k, h, target, 2, sib, sib_sem)

    def finish(n):
        k, h = steps[n]
        arrived(k, h, corner)
        if (k + 1, h) in CLIMB:
            rise(k, h, corner, 1)
        give(k, h, corner, 3, sib, sib_sem)

    def gather(n):
        k, h = steps[n]
        for slot in held:
            arrived(k, h, slot + 1 - 2 * lax.rem(slot, 2))

    size = 2 * segs * GROUP
    few = GROUP // 2
    same = (lax.broadcasted_iota(jnp.int32, (channels * few, size), 0) % few
            == lax.broadcasted_iota(jnp.int32, (channels * few, size), 1) % few)

    def build(q, carry):
        at = pl.multiple_of(q * size, size)
        first = buf[0, g, :, pl.ds(at, size)].astype(jnp.float32)
        second = jnp.concatenate([first[:, LANES:], -first[:, :LANES]], axis=1)
        for i, value in enumerate((first, second)):
            wide = jnp.broadcast_to(value[:, None, :], (channels, few, size)).reshape(channels * few, size)
            diag[q, i * channels * few:(i + 1) * channels * few, :] = jnp.where(same, wide, 0.0).astype(jnp.bfloat16)
        return carry

    block = grps * channels
    upper = lax.broadcasted_iota(jnp.int32, (block, size), 1) % GROUP >= few

    def multiply(q, k):
        other = buf[k, :, :, q * size:(q + 1) * size].reshape(block, size)
        zero = jnp.zeros_like(other)
        other = jnp.concatenate([jnp.where(upper, zero, other), jnp.where(upper, other, zero)], axis=0)
        product = mm_t(diag[q], other).reshape(2, 2, pair, few, 2 * block)
        product = jnp.concatenate([product[..., :block], product[..., block:]], axis=3).astype(jnp.bfloat16)
        for i in range(2):
            for p in range(2):
                cross[:, i, q * GROUP:(q + 1) * GROUP, p * block:(p + 1) * block] = product[i, p]

    begun = early_bins(half)

    def early(j):
        if begun:
            for c in range(j * pair // 2, (j + 1) * pair // 2):
                acc[c] = mm(columns(lag_ref, half, 0, begun), cross[c, :, :begun].reshape(2 * begun, 2 * block))

    def lag(c):
        total = mm(lag_ref[...], cross[c].reshape(2 * half, 2 * block))
        if normalise:
            total = total * inv[c:c + 1, :]
        stage[pl.ds(c, LAGS, stride=channels), :] = total[:, :block]
        stage[pl.ds(c + pair, LAGS, stride=channels), :] = total[:, block:]

    def place(k):
        for n in range(LAGS // 16):
            part = stage[n * 16 * channels:(n + 1) * 16 * channels, :]
            out_ref[n * 16:(n + 1) * 16, k] = part.astype(jnp.bfloat16).reshape(16, channels, block)

    def prepare(n):
        lax.fori_loop(bounds[n], bounds[n + 1], build, 0, unroll=2)

    def combine(n):
        k, h = steps[n]
        gather(n)
        for q in range(bounds[h], bounds[h + 1]):
            multiply(q, k)

    def emit(n):
        k = n // 2
        if n == 0:
            loads[-1].wait()
        if n % 2 == 0:
            tile = buf[k, :, :, width:width + LANES].reshape(block, LANES)
            count = mm_t(flags.astype(jnp.bfloat16), tile)
            count_ref[:, k * block:(k + 1) * block] = count
            factor = lax.rsqrt(bins * jnp.maximum(count, 1.0))
            inv[:, :block] = factor[:pair]
            inv[:, block:] = factor[pair:]
        if k < STEPS - 1:
            for c in range(n % 2 * pair // 2, (n % 2 + 1) * pair // 2):
                lag(c)

    acts = {"s": spread, "f": forward, "t": relay, "c": finish, "b": prepare, "m": combine, "e": emit, "g": early, "p": place}
    for act, n in ORDER:
        acts[act](n)

    for copy in sent:
        copy.wait_send()


def last_kernel(normalise, first_ref, cross, acc, inv, lag_ref, out_hbm, stage, tail, sems):
    pair, half = cross.shape[0], cross.shape[2]
    channels, block = 2 * pair, cross.shape[3] // 2
    begun = early_bins(half)
    first = pltpu.make_async_copy(first_ref, out_hbm.at[:, pl.ds(0, STEPS - 1)], sems.at[LAST])
    first.start()
    for c in range(pair):
        total = mm(columns(lag_ref, half, begun, half), cross[c, :, begun:].reshape(2 * (half - begun), 2 * block))
        if begun:
            total = acc[c] + total
        if normalise:
            total = total * inv[c:c + 1, :]
        stage[pl.ds(c, LAGS, stride=channels), :] = total[:, :block]
        stage[pl.ds(c + pair, LAGS, stride=channels), :] = total[:, block:]
    span = LAGS // LAST
    copies = []
    for m in range(LAST):
        for n in range(m * span // 16, (m + 1) * span // 16):
            part = stage[n * 16 * channels:(n + 1) * 16 * channels, :]
            tail[n * 16:(n + 1) * 16] = part.astype(jnp.bfloat16).reshape(16, channels, block)
        rows = pl.ds(m * span, span)
        copies.append(pltpu.make_async_copy(tail.at[rows], out_hbm.at[rows, STEPS - 1], sems.at[m]))
        copies[-1].start()
    for copy in copies + [first]:
        copy.wait()


def on_device(records, flags):
    channels, segs, length = records.shape
    bins = length // 2
    splits = lax.axis_size("sub")
    blks = lax.axis_size("blk")
    grps = lax.axis_size("grp")
    half = bins // splits
    block = grps * channels
    cos, sin = dft_tables(length)
    lags = lag_tables(length)
    both = np.stack([cos, sin], axis=1)
    high = both.astype(ml_dtypes.bfloat16)
    high, lags = jnp.asarray(high), jnp.asarray(lags)
    if splits > 1:
        first = lax.axis_index("sub") * half
        high = jnp.roll(high, -first, axis=2)
        lags = lax.dynamic_slice_in_dim(lags, first, half, 2)
    width = half * 2 * segs + LANES
    vmem = pl.BlockSpec(memory_space=pltpu.VMEM)
    first, cross, acc, inv, lags, count = pl.pallas_call(
        functools.partial(kernel, blks, grps, (channels, segs, bins, half), splits == 1),
        out_shape=(
            pltpu.VMEM((LAGS, STEPS - 1, channels, block), jnp.bfloat16),
            pltpu.VMEM((channels // 2, 2, half, 2 * block), jnp.bfloat16),
            pltpu.VMEM((channels // 2, LAGS, 2 * block), jnp.float32),
            pltpu.VMEM((channels // 2, 2 * block), jnp.float32),
            pltpu.VMEM((LAGS, 2 * half), jnp.bfloat16),
            pltpu.VMEM((channels, STEPS * block), jnp.float32),
        ),
        in_specs=[pl.BlockSpec(memory_space=pltpu.HBM)] * 4,
        out_specs=(vmem,) * 6,
        scratch_shapes=[
            pltpu.VMEM((channels * segs, length), jnp.bfloat16),
            pltpu.VMEM((segs, channels), jnp.int32),
            pltpu.VMEM((length, 2 * bins), jnp.bfloat16),
            pltpu.VMEM((segs * LANES, segs * LANES), jnp.bfloat16),
            pltpu.SemaphoreType.DMA((3 + TURNS,)),
            pltpu.VMEM((STEPS, grps, channels, width), jnp.bfloat16),
            pltpu.VMEM((half // GROUP, channels * GROUP, 2 * segs * GROUP), jnp.bfloat16),
            pltpu.VMEM((channels, LANES), jnp.float32),
            pltpu.VMEM(((LAGS + 1) * channels, block), jnp.float32),
            pltpu.SemaphoreType.DMA((STEPS, PIECES, grps)),
            pltpu.SemaphoreType.DMA((STEPS - 1, PIECES, 2)),
            pltpu.SemaphoreType.DMA((STEPS, PIECES, 3)),
            pltpu.SemaphoreType.DMA((STEPS, PIECES, grps // 2)),
        ],
        compiler_params=pltpu.CompilerParams(
            collective_id=0, has_side_effects=True, vmem_limit_bytes=54 * 1024 * 1024
        ),
    )(
        records.reshape(channels * segs, length),
        flags.T,
        high.reshape(length, 2 * bins),
        lags.reshape(LAGS, 2 * half),
    )
    out = pl.pallas_call(
        functools.partial(last_kernel, splits == 1),
        out_shape=jax.ShapeDtypeStruct((LAGS, STEPS, channels, block), jnp.bfloat16),
        in_specs=[vmem] * 5,
        out_specs=pl.BlockSpec(memory_space=pltpu.HBM),
        scratch_shapes=[
            pltpu.VMEM(((LAGS + 1) * channels, block), jnp.float32),
            pltpu.VMEM((LAGS, channels, block), jnp.bfloat16),
            pltpu.SemaphoreType.DMA((LAST + 1,)),
        ],
        compiler_params=pltpu.CompilerParams(vmem_limit_bytes=32 * 1024 * 1024),
    )(first, cross, acc, inv, lags)
    out = out.transpose(0, 2, 1, 3)
    if splits > 1:
        out = lax.psum_scatter(out, "sub", scatter_dimension=0, tiled=True).astype(jnp.float32)
        out = (out / jnp.sqrt(bins * jnp.maximum(count, 1.0)).reshape(1, channels, STEPS, block)).astype(jnp.bfloat16)
    return out


def solution(mesh):
    return jax.shard_map(
        on_device,
        mesh=mesh,
        in_specs=(P(("dom", "blk", "grp"), None, None), P(("dom", "blk", "grp"), None)),
        out_specs=P("sub", ("dom", "blk", "grp"), None, None),
        check_vma=False,
    )
```

```python
import functools

import jax
import jax.numpy as jnp
import ml_dtypes
import numpy as np
from jax import lax
from jax.experimental import pallas as pl
from jax.experimental.pallas import tpu as pltpu
from jax.sharding import PartitionSpec as P

LAGS = 256
STEPS = 3
LANES = 128
GROUP = 16
TURNS = 4
SPLIT = (0, 1, 2)
LAST = 4
PIECES = len(SPLIT) - 1
CLIMB = ((1, 0), (1, 1), (2, 0))
ORDER = (
    ("s", 0), ("s", 1), ("f", 0), ("t", 0), ("b", 0), ("s", 2), ("f", 1), ("s", 3), ("c", 0), ("m", 0), ("s", 4), ("t", 1), ("f", 2), ("c", 1), ("t", 2), ("s", 5), ("b", 1), ("c", 2), ("m", 1), ("t", 3), ("f", 3), ("e", 0), ("e", 1), ("p", 0), ("c", 3), ("f", 4), ("m", 2), ("t", 4), ("t", 5), ("f", 5), ("m", 3), ("c", 4), ("e", 2), ("e", 3), ("p", 1), ("c", 5), ("m", 4), ("g", 0), ("g", 1), ("m", 5), ("e", 4),
)
MESH = pl.DeviceIdType.MESH


def dft_tables(length):
    bins = length // 2
    phase = np.mod(np.arange(length)[:, None] * np.arange(bins)[None, :], length)
    angle = 2.0 * np.pi * phase / length
    return np.cos(angle).astype(np.float32), (-np.sin(angle)).astype(np.float32)


def lag_tables(length):
    bins = length // 2
    phase = np.mod((np.arange(LAGS) - LAGS // 2)[:, None] * np.arange(bins)[None, :], length)
    angle = 2.0 * np.pi * phase / length
    both = np.stack([np.cos(angle), -np.sin(angle)], axis=1).astype(np.float32)
    return both.astype(ml_dtypes.bfloat16)


def early_bins(half):
    return half // GROUP * SPLIT[-2] // SPLIT[-1] * GROUP // LANES * LANES


def columns(ref, half, low, high):
    return jnp.concatenate([ref[:, i * half + low:i * half + high] for i in range(2)], axis=1)


def mm(a, b):
    return jnp.dot(a, b, preferred_element_type=jnp.float32)


def mm_t(a, b):
    return lax.dot_general(a, b, (((1,), (1,)), ((), ())), preferred_element_type=jnp.float32)


def kernel(
    blks, grps, dims, normalise,
    rec_hbm, flag_hbm, hi_hbm, lag_hbm,
    out_ref, cross, acc, inv, lag_ref, count_ref,
    rec_ref, flag_ref, hi_ref, perm_ref, load_sem, buf, diag, wide, stage, recv_sem, hop_sem, peer_sem, sib_sem,
):
    channels, segs, bins, half = dims
    width = half * 2 * segs
    chunks = half // GROUP
    pair = channels // 2
    depth = hi_hbm.shape[0] // TURNS
    parts = [pl.ds(n * depth, depth) for n in range(TURNS)]
    loads = [
        pltpu.make_async_copy(source, target, load_sem.at[n])
        for n, (source, target) in enumerate(
            [(rec_hbm, rec_ref), (flag_hbm, flag_ref)]
            + [(hi_hbm.at[rows], hi_ref.at[rows]) for rows in parts] + [(lag_hbm, lag_ref)])
    ]
    for load in loads[:-1]:
        load.start()
    b = lax.axis_index("blk")
    g = lax.axis_index("grp")
    sib = g + 1 - 2 * lax.rem(g, 2)
    core = lax.rem(g, 2)
    across = g + 2 - 4 * lax.rem(g // 2, 2)
    along = g + 4 - 8 * lax.rem(g // 4, 2)
    source = (1 - core) * across + core * along
    target = core * across + (1 - core) * along
    corner = across + along - g
    held = (g, source, target, corner)

    barrier = pltpu.get_barrier_semaphore()
    pl.semaphore_signal(barrier, inc=1, device_id={"blk": lax.rem(b + blks - 1, blks)}, device_id_type=MESH)
    for other in (across, along, sib):
        pl.semaphore_signal(barrier, inc=1, device_id={"grp": other}, device_id_type=MESH)

    per = LANES // GROUP
    came = lax.broadcasted_iota(jnp.int32, (segs * LANES, 1), 0)
    goes = came // GROUP % per * LANES + came // LANES * GROUP + came % GROUP
    lane = lax.broadcasted_iota(jnp.int32, (segs * LANES, LANES), 1)
    for q in range(per):
        perm_ref[:, q * LANES:(q + 1) * LANES] = jnp.where(goes == lane + q * LANES, 1.0, 0.0).astype(jnp.bfloat16)
    came = lax.broadcasted_iota(jnp.int32, (segs * channels, segs * channels), 0)
    goes = came % channels * segs + came // channels
    order = jnp.where(goes == lax.broadcasted_iota(jnp.int32, came.shape, 1), 1.0, 0.0).astype(jnp.bfloat16)
    loads[0].wait()
    rec = mm(order, rec_ref[...]).astype(jnp.bfloat16)
    spec = 0.0
    for n in range(TURNS):
        loads[2 + n].wait()
        spec = spec + mm(rec[:, n * depth:(n + 1) * depth], hi_ref[parts[n]])
    loads[1].wait()
    real = spec[:, :bins]
    imag = spec[:, bins:]
    power = real * real + imag * imag
    level = jnp.sum(power, axis=1, keepdims=True) / bins
    scale = 1.0 / jnp.sqrt(power[:, :half] + level + 1e-06)
    wide[...] = jnp.zeros_like(wide)
    unit = (lax.broadcasted_iota(jnp.int32, (channels, channels), 0)
            == lax.broadcasted_iota(jnp.int32, (channels, channels), 1)).astype(jnp.float32)
    wide[:, :segs] = mm_t(unit, flag_ref[...].astype(jnp.float32))
    flags = wide[...]
    pieces = [(real[:, :half] * scale).astype(jnp.bfloat16), (imag[:, :half] * scale).astype(jnp.bfloat16)]
    rows = []
    for t in range(half // LANES):
        for piece in pieces:
            rows.append(jnp.concatenate([
                piece[s * channels:(s + 1) * channels, t * LANES:(t + 1) * LANES]
                * flags[:, s:s + 1].astype(jnp.bfloat16)
                for s in range(segs)
            ], axis=1))
    regrouped = mm(jnp.concatenate(rows, axis=0), perm_ref[...]).astype(jnp.bfloat16)
    for t in range(half // LANES):
        for i in range(2):
            part = regrouped[(t * 2 + i) * channels:(t * 2 + i + 1) * channels]
            for q in range(per):
                at = ((t * per + q) * 2 + i) * LANES
                buf[0, g, :, at:at + LANES] = part[:, q * LANES:(q + 1) * LANES]
    buf[0, g, :, width:width + LANES] = flags.astype(jnp.bfloat16)

    loads[-1].start()
    pl.semaphore_wait(barrier, 4)

    sent = []

    bounds = [chunks * part // SPLIT[-1] for part in SPLIT]
    edges = [2 * segs * GROUP * bound for bound in bounds[:-1]] + [width + LANES]
    spans = [(low, high - low) for low, high in zip(edges[:-1], edges[1:])]
    steps = [(k, h) for k in range(STEPS) for h in range(PIECES)]

    def piece(k, h, slot):
        return buf.at[k, slot, :, pl.ds(*spans[h])]

    def send(source, target, send_sem, landed, where):
        copy = pltpu.make_async_remote_copy(
            src_ref=source, dst_ref=target, send_sem=send_sem, recv_sem=landed,
            device_id=where, device_id_type=MESH,
        )
        copy.start()
        sent.append(copy)

    def arrived(k, h, slot):
        ref = piece(k, h, slot)
        pltpu.make_async_copy(ref, ref, recv_sem.at[k, h, slot]).wait()

    def give(k, h, slot, n, other, sem):
        ref = piece(k, h, slot)
        send(ref, ref, sem.at[k, h, n], recv_sem.at[k, h, slot], {"grp": other})

    def rise(k, h, slot, n):
        send(piece(k, h, slot), piece(k + 1, h, slot), hop_sem.at[k, h, n], recv_sem.at[k + 1, h, slot],
             {"blk": lax.rem(b + 1, blks)})

    def spread(n):
        k, h = steps[n]
        if k:
            arrived(k, h, g)
        give(k, h, g, 0, target, peer_sem)
        give(k, h, g, 1, source, peer_sem)
        if k + 1 < STEPS:
            rise(k, h, g, 0)
        give(k, h, g, 0, sib, sib_sem)

    def forward(n):
        k, h = steps[n]
        arrived(k, h, source)
        if (k, h) not in CLIMB:
            give(k, h, source, 2, target, peer_sem)
        give(k, h, source, 1, sib, sib_sem)

    def relay(n):
        k, h = steps[n]
        arrived(k, h, target)
        give(k, h, target, 2, sib, sib_sem)

    def finish(n):
        k, h = steps[n]
        arrived(k, h, corner)
        if (k + 1, h) in CLIMB:
            rise(k, h, corner, 1)
        give(k, h, corner, 3, sib, sib_sem)

    def gather(n):
        k, h = steps[n]
        for slot in held:
            arrived(k, h, slot + 1 - 2 * lax.rem(slot, 2))

    size = 2 * segs * GROUP
    few = GROUP // 2
    same = (lax.broadcasted_iota(jnp.int32, (channels * few, size), 0) % few
            == lax.broadcasted_iota(jnp.int32, (channels * few, size), 1) % few)

    def build(q, carry):
        at = pl.multiple_of(q * size, size)
        first = buf[0, g, :, pl.ds(at, size)].astype(jnp.float32)
        second = jnp.concatenate([first[:, LANES:], -first[:, :LANES]], axis=1)
        for i, value in enumerate((first, second)):
            wide = jnp.broadcast_to(value[:, None, :], (channels, few, size)).reshape(channels * few, size)
            diag[q, i * channels * few:(i + 1) * channels * few, :] = jnp.where(same, wide, 0.0).astype(jnp.bfloat16)
        return carry

    block = grps * channels
    upper = lax.broadcasted_iota(jnp.int32, (block, size), 1) % GROUP >= few

    def multiply(q, k):
        other = buf[k, :, :, q * size:(q + 1) * size].reshape(block, size)
        zero = jnp.zeros_like(other)
        other = jnp.concatenate([jnp.where(upper, zero, other), jnp.where(upper, other, zero)], axis=0)
        product = mm_t(diag[q], other).reshape(2, 2, pair, few, 2 * block)
        product = jnp.concatenate([product[..., :block], product[..., block:]], axis=3).astype(jnp.bfloat16)
        for i in range(2):
            for p in range(2):
                cross[:, i, q * GROUP:(q + 1) * GROUP, p * block:(p + 1) * block] = product[i, p]

    begun = early_bins(half)

    def early(j):
        if begun:
            for c in range(j * pair // 2, (j + 1) * pair // 2):
                acc[c] = mm(columns(lag_ref, half, 0, begun), cross[c, :, :begun].reshape(2 * begun, 2 * block))

    def lag(c):
        total = mm(lag_ref[...], cross[c].reshape(2 * half, 2 * block))
        if normalise:
            total = total * inv[c:c + 1, :]
        stage[pl.ds(c, LAGS, stride=channels), :] = total[:, :block]
        stage[pl.ds(c + pair, LAGS, stride=channels), :] = total[:, block:]

    def place(k):
        for n in range(LAGS // 16):
            part = stage[n * 16 * channels:(n + 1) * 16 * channels, :]
            out_ref[n * 16:(n + 1) * 16, k] = part.astype(jnp.bfloat16).reshape(16, channels, block)

    def prepare(n):
        lax.fori_loop(bounds[n], bounds[n + 1], build, 0, unroll=2)

    def combine(n):
        k, h = steps[n]
        gather(n)
        for q in range(bounds[h], bounds[h + 1]):
            multiply(q, k)

    def emit(n):
        k = n // 2
        if n == 0:
            loads[-1].wait()
        if n % 2 == 0:
            tile = buf[k, :, :, width:width + LANES].reshape(block, LANES)
            count = mm_t(flags.astype(jnp.bfloat16), tile)
            count_ref[:, k * block:(k + 1) * block] = count
            factor = lax.rsqrt(bins * jnp.maximum(count, 1.0))
            inv[:, :block] = factor[:pair]
            inv[:, block:] = factor[pair:]
        if k < STEPS - 1:
            for c in range(n % 2 * pair // 2, (n % 2 + 1) * pair // 2):
                lag(c)

    acts = {"s": spread, "f": forward, "t": relay, "c": finish, "b": prepare, "m": combine, "e": emit, "g": early, "p": place}
    for act, n in ORDER:
        acts[act](n)

    for copy in sent:
        copy.wait_send()


def last_kernel(normalise, first_ref, cross, acc, inv, lag_ref, out_hbm, stage, tail, sems):
    pair, half = cross.shape[0], cross.shape[2]
    channels, block = 2 * pair, cross.shape[3] // 2
    begun = early_bins(half)
    first = pltpu.make_async_copy(first_ref, out_hbm.at[:, pl.ds(0, STEPS - 1)], sems.at[LAST])
    first.start()
    for c in range(pair):
        total = mm(columns(lag_ref, half, begun, half), cross[c, :, begun:].reshape(2 * (half - begun), 2 * block))
        if begun:
            total = acc[c] + total
        if normalise:
            total = total * inv[c:c + 1, :]
        stage[pl.ds(c, LAGS, stride=channels), :] = total[:, :block]
        stage[pl.ds(c + pair, LAGS, stride=channels), :] = total[:, block:]
    span = LAGS // LAST
    copies = []
    for m in range(LAST):
        for n in range(m * span // 16, (m + 1) * span // 16):
            part = stage[n * 16 * channels:(n + 1) * 16 * channels, :]
            tail[n * 16:(n + 1) * 16] = part.astype(jnp.bfloat16).reshape(16, channels, block)
        rows = pl.ds(m * span, span)
        copies.append(pltpu.make_async_copy(tail.at[rows], out_hbm.at[rows, STEPS - 1], sems.at[m]))
        copies[-1].start()
    for copy in copies + [first]:
        copy.wait()


def on_device(records, flags):
    channels, segs, length = records.shape
    bins = length // 2
    splits = lax.axis_size("sub")
    blks = lax.axis_size("blk")
    grps = lax.axis_size("grp")
    half = bins // splits
    block = grps * channels
    cos, sin = dft_tables(length)
    lags = lag_tables(length)
    both = np.stack([cos, sin], axis=1)
    high = both.astype(ml_dtypes.bfloat16)
    high, lags = jnp.asarray(high), jnp.asarray(lags)
    if splits > 1:
        first = lax.axis_index("sub") * half
        high = jnp.roll(high, -first, axis=2)
        lags = lax.dynamic_slice_in_dim(lags, first, half, 2)
    width = half * 2 * segs + LANES
    vmem = pl.BlockSpec(memory_space=pltpu.VMEM)
    first, cross, acc, inv, lags, count = pl.pallas_call(
        functools.partial(kernel, blks, grps, (channels, segs, bins, half), splits == 1),
        out_shape=(
            pltpu.VMEM((LAGS, STEPS - 1, channels, block), jnp.bfloat16),
            pltpu.VMEM((channels // 2, 2, half, 2 * block), jnp.bfloat16),
            pltpu.VMEM((channels // 2, LAGS, 2 * block), jnp.float32),
            pltpu.VMEM((channels // 2, 2 * block), jnp.float32),
            pltpu.VMEM((LAGS, 2 * half), jnp.bfloat16),
            pltpu.VMEM((channels, STEPS * block), jnp.float32),
        ),
        in_specs=[pl.BlockSpec(memory_space=pltpu.HBM)] * 4,
        out_specs=(vmem,) * 6,
        scratch_shapes=[
            pltpu.VMEM((channels * segs, length), jnp.bfloat16),
            pltpu.VMEM((segs, channels), jnp.int32),
            pltpu.VMEM((length, 2 * bins), jnp.bfloat16),
            pltpu.VMEM((segs * LANES, segs * LANES), jnp.bfloat16),
            pltpu.SemaphoreType.DMA((3 + TURNS,)),
            pltpu.VMEM((STEPS, grps, channels, width), jnp.bfloat16),
            pltpu.VMEM((half // GROUP, channels * GROUP, 2 * segs * GROUP), jnp.bfloat16),
            pltpu.VMEM((channels, LANES), jnp.float32),
            pltpu.VMEM(((LAGS + 1) * channels, block), jnp.float32),
            pltpu.SemaphoreType.DMA((STEPS, PIECES, grps)),
            pltpu.SemaphoreType.DMA((STEPS - 1, PIECES, 2)),
            pltpu.SemaphoreType.DMA((STEPS, PIECES, 3)),
            pltpu.SemaphoreType.DMA((STEPS, PIECES, grps // 2)),
        ],
        compiler_params=pltpu.CompilerParams(
            collective_id=0, has_side_effects=True, vmem_limit_bytes=54 * 1024 * 1024
        ),
    )(
        records.reshape(channels * segs, length),
        flags.T,
        high.reshape(length, 2 * bins),
        lags.reshape(LAGS, 2 * half),
    )
    out = pl.pallas_call(
        functools.partial(last_kernel, splits == 1),
        out_shape=jax.ShapeDtypeStruct((LAGS, STEPS, channels, block), jnp.bfloat16),
        in_specs=[vmem] * 5,
        out_specs=pl.BlockSpec(memory_space=pltpu.HBM),
        scratch_shapes=[
            pltpu.VMEM(((LAGS + 1) * channels, block), jnp.float32),
            pltpu.VMEM((LAGS, channels, block), jnp.bfloat16),
            pltpu.SemaphoreType.DMA((LAST + 1,)),
        ],
        compiler_params=pltpu.CompilerParams(vmem_limit_bytes=32 * 1024 * 1024),
    )(first, cross, acc, inv, lags)
    out = out.transpose(0, 2, 1, 3)
    if splits > 1:
        out = lax.psum_scatter(out, "sub", scatter_dimension=0, tiled=True).astype(jnp.float32)
        out = (out / jnp.sqrt(bins * jnp.maximum(count, 1.0)).reshape(1, channels, STEPS, block)).astype(jnp.bfloat16)
    return out


def solution(mesh):
    return jax.shard_map(
        on_device,
        mesh=mesh,
        in_specs=(P(("dom", "blk", "grp"), None, None), P(("dom", "blk", "grp"), None)),
        out_specs=P("sub", ("dom", "blk", "grp"), None, None),
        check_vma=False,
    )
```
